512 devices in a mesh: space: 32 (over z_lo, y, core), mode: 16 (over z_hi, x).
Axes of the slice: x: 4, y: 8, z: 8 (z_hi: 4, z_lo: 2; z = z_hi * 2 + z_lo), core: 2. Of those that a mesh axis runs over, the one named last changes fastest.
Arguments:
- occupation_deviation: float32 [2048, 64, 4, 128], P('mode', 'space'), may hold values from -6 to 6
- initial_thermal_offset: float32 [64, 4, 128], P('space'), may hold values from -6 to 6
- branch_specific_warmth: float32 [2048], replicated, may hold values from 0.2 to 2
- courant_numbers: float32 [3, 2048], P(None, 'mode'), may hold values from 0.02 to 0.3
- sign_quadrant: int32 [2048], P('mode'), may hold values from 0 to 7
- scattering_matrix: bfloat16 [2048, 2048], P('mode'), may hold values from -1 to 1
Outputs:
- population_out: float32 [2048, 64, 4, 128], P('mode', 'space')
- thermal_offset: float32 [64, 4, 128], P('space')
The draws below stay inside these ranges and needn't reach their ends.
All inputs are finite; a program needn't handle non-finite values.
Results may differ from the reference program's by a relative error of at most 0.002.
Values may be sent and summed in bfloat16 or wider, within the bound.
A program may use at most 64 MiB of HBM per device.

```python
import math
import jax
import jax.numpy as jnp
from jax import lax

M = 2048
GRID_LENGTH_TWO = 4
GRID_LENGTH_THREE = 128
ITERS = 3
GRID_LENGTH_ONE = 64


def draw_scattering_matrix(key, part):
    key_diag, key_off = jax.random.split(jax.random.fold_in(key, 17))
    diag_values = jnp.exp(jax.random.uniform(key_diag, (M,), jnp.float32, jnp.log(0.3), jnp.log(0.8)))
    off_part = jax.random.normal(key_off, (M, M), jnp.float32) * (0.25 / jnp.sqrt(M * 1.0))
    return (off_part + jnp.diag(diag_values)).astype(jnp.bfloat16)


def touch_ends(array, stream_key, least, top_value):
    longest = array.shape.index(max(array.shape))
    spots = []
    for shift in (0, 1):
        where = [jax.random.randint(jax.random.fold_in(stream_key, axis), (), 0, length) for axis, length in enumerate(array.shape)]
        where[longest] = (where[longest] + shift) % array.shape[longest]
        spots.append(tuple(where))
    return array.at[spots[0]].set(least).at[spots[1]].set(top_value)


def levels(rng, extent, cuts, smallest, largest):
    loudness = 1.0
    for position, shards_of in cuts:
        steps = jax.random.uniform(jax.random.fold_in(jax.random.fold_in(rng, 6), position), (shards_of,), jnp.float32, smallest / len(cuts), largest / len(cuts))
        loudness = loudness * jnp.repeat(jnp.exp(steps), extent[position] // shards_of).reshape((-1,) + (1,) * (len(extent) - 1 - position))
    return loudness


def gaussian(stream_key, dims, spread, most, cuts=(), kind=jnp.bfloat16):
    array = spread * jax.random.normal(stream_key, dims, jnp.float32)
    if cuts:
        array = array * levels(stream_key, dims, cuts, -0.22, 0.18)
    return jnp.clip(array, -most, most).astype(kind)


def setup_inputs(seed: int = 0) -> dict:
    seeds = jax.random.split(jax.random.key(seed), 7)
    occupation_deviation = gaussian(seeds[0], (M, GRID_LENGTH_ONE, GRID_LENGTH_TWO, GRID_LENGTH_THREE), 1.0, 6.0, ((0, 16), (1, 32)), jnp.float32)
    initial_thermal_offset = gaussian(seeds[1], (GRID_LENGTH_ONE, GRID_LENGTH_TWO, GRID_LENGTH_THREE), 1.0, 6.0, ((0, 32),), jnp.float32)
    branch_specific_warmth = jnp.clip(jnp.exp(jax.random.uniform(seeds[2], (M,), jnp.float32, math.log(0.2), math.log(2.0))), 0.2, 2.0)
    courant_numbers = jnp.clip(jnp.exp(math.log(0.3) - 2.7080503 * jax.random.uniform(seeds[3], (3, M), jnp.float32) ** levels(seeds[3], (3, M), ((1, 16),), -0.2, 0.2)), 0.02, 0.3)
    sign_quadrant = touch_ends(jax.random.randint(seeds[4], (M,), 0, 8), jax.random.fold_in(seeds[4], 1), 0, 7).astype(jnp.int32)
    scattering_matrix = draw_scattering_matrix(jax.random.fold_in(seeds[6], 71), 0)
    return {"occupation_deviation": occupation_deviation, "initial_thermal_offset": initial_thermal_offset, "branch_specific_warmth": branch_specific_warmth, "courant_numbers": courant_numbers, "sign_quadrant": sign_quadrant, "scattering_matrix": scattering_matrix}


def advect(lattice_wave_carry, courant_numbers, sign_quadrant):
    advected = lattice_wave_carry
    for dim_index in range(3):
        grid_axis = dim_index + 1
        below_side = jnp.roll(lattice_wave_carry, 1, grid_axis)
        above_side = jnp.roll(lattice_wave_carry, -1, grid_axis)
        sign_bit = ((sign_quadrant >> dim_index) & 1).reshape(-1, 1, 1, 1)
        upwind = jnp.where(sign_bit == 1, above_side, below_side)
        advected = advected - courant_numbers[dim_index].reshape(-1, 1, 1, 1) * (lattice_wave_carry - upwind)
    return advected


def reference(occupation_deviation, initial_thermal_offset, branch_specific_warmth, courant_numbers, sign_quadrant, scattering_matrix):
    summed_specific_warmth = jnp.sum(branch_specific_warmth)
    lattice_wave_carry = occupation_deviation + branch_specific_warmth.reshape(-1, 1, 1, 1) * initial_thermal_offset[None]
    scattering_source = jnp.dot(scattering_matrix.astype(jnp.float32), branch_specific_warmth, precision=lax.Precision.HIGHEST)
    partition_extents = occupation_deviation.shape
    thermal_offset = jnp.zeros(partition_extents[1:], jnp.float32)
    for iteration in range(ITERS):
        upstream_occupation = advect(lattice_wave_carry, courant_numbers, sign_quadrant)
        moved_bf = upstream_occupation.astype(jnp.bfloat16)
        flat_rows = moved_bf.reshape(partition_extents[0], -1)
        internal_warmth_field = jnp.dot(branch_specific_warmth, flat_rows.astype(jnp.float32), precision=lax.Precision.HIGHEST)
        thermal_offset = (internal_warmth_field / summed_specific_warmth).reshape(partition_extents[1:])
        scattering_applied = jnp.dot(scattering_matrix, flat_rows, preferred_element_type=jnp.float32).reshape(partition_extents)
        lattice_wave_carry = upstream_occupation - scattering_applied + scattering_source.reshape(-1, 1, 1, 1) * thermal_offset[None]
    return lattice_wave_carry, thermal_offset
```

```python
import functools

import jax
import jax.numpy as jnp
from jax import lax
from jax.experimental import pallas as pl
from jax.experimental.pallas import tpu as pltpu
from jax.sharding import PartitionSpec as P

ITERS = 3
NA, NB = 4, 4
NK = NA * NB
NS = 32
MODES = 128
M = NK * MODES
MESH = pl.DeviceIdType.MESH

SLOTS = [
    ("p", 0), ("r", 0, 0), ("p", 1), ("r", 0, 1), ("p", 2), ("r", 0, 2), ("r", 1, 0), ("r", 0, 3),
    ("r", 1, 1), ("r", 1, 2), ("r", 2, 0), ("r", 1, 3), ("r", 2, 1), ("r", 2, 2), ("r", 2, 3),
]
SEQ = {item: n for n, item in enumerate(SLOTS)}


def kernel(
    occ_ref, t0_ref, warm_ref, cour_ref, sign_ref, s_ref,
    out_ref, therm_ref,
    full, sent, state, final, landed, lhs, wlhs, relax, xs, xr, zs, zr, moved,
    own_sem, g_send, g_recv, c_send, c_recv, in_send, in_recv, x_send, x_recv, z_send, z_recv, o_send, o_recv,
):
    s = lax.axis_index("space")
    k = lax.axis_index("mode")
    a, b = k // NB, k % NB
    lo = s // 16
    core = s % 2

    def dev(space, mode):
        return {"space": space, "mode": mode}

    def wrap(v, n):
        return lax.rem(v + 4 * n, n)

    def x_peer(sg):
        return dev(s, a * NB + wrap(b + sg, NB))

    def z_peer(sg):
        crosses = lo if sg > 0 else 1 - lo
        return dev(lax.rem(s + 16, NS), wrap(a + sg * crosses, NA) * NB + b)

    partner = dev(s + 1 - 2 * core, k)
    right, left = dev(wrap(s + 1, NS), k), dev(wrap(s - 1, NS), k)
    z_next, z_prev = dev(s, wrap(k + 1, NK)), dev(s, wrap(k - 1, NK))

    def mode_peer(d):
        return wrap(k + d, NK)

    own = pltpu.make_async_copy(s_ref, full.at[a, b], own_sem)
    own.start()
    barrier = pltpu.get_barrier_semaphore()

    @pl.loop(1, NK)
    def _(d):
        pl.semaphore_signal(barrier, inc=1, device_id=dev(s, mode_peer(d)), device_id_type=MESH)

    for peer in (right, left, z_peer(1), z_peer(-1)):
        pl.semaphore_signal(barrier, inc=1, device_id=peer, device_id_type=MESH)

    warm_col = jnp.transpose(jnp.broadcast_to(warm_ref[pl.ds(k, 1), :], (MODES, MODES)))
    for xy in range(8):
        cells = occ_ref[pl.ds(xy, MODES, stride=8), :] + warm_col * t0_ref[xy:xy + 1, :]
        sent[:, pl.ds(xy * 8, 8), :] = jnp.transpose(cells).reshape(NK, 8, MODES)
    sign = sign_ref[...]
    row = lax.broadcasted_iota(jnp.int32, (8, MODES), 0)
    coef = jnp.zeros((8, MODES), jnp.float32)
    for d in range(3):
        bit = jnp.broadcast_to((sign >> d) & 1, (8, MODES))
        c = jnp.broadcast_to(cour_ref[d:d + 1, :], (8, MODES))
        coef = jnp.where(row == 2 * d, jnp.where(bit == 0, c, 0.0), coef)
        coef = jnp.where(row == 2 * d + 1, jnp.where(bit == 1, c, 0.0), coef)
    sent[:, 64:72, :] = jnp.broadcast_to(coef[None], (NK, 8, MODES))

    pl.semaphore_wait(barrier, NK - 1 + 4)

    def a2a(src, dst, send, recv, d):
        there = mode_peer(d)
        return pltpu.make_async_remote_copy(
            src_ref=src.at[there], dst_ref=dst.at[k], send_sem=send.at[d], recv_sem=recv.at[d],
            device_id=dev(s, there), device_id_type=MESH,
        )

    @pl.loop(1, NK)
    def _(d):
        a2a(sent, state, in_send, in_recv, d).start()

    state[k] = sent[k]

    own.wait()

    def piece(link, sg, item):
        color = (0 if sg > 0 else 1) if (link == "x") == (item[0] == "r") else (2 if sg > 0 else 3)
        return color

    def z_from(sg, i):
        follows = (1 - lo) if sg > 0 else lo
        return wrap(a - sg * (i + follows), NA)

    def x_from(sg, i):
        return wrap(b - sg * i, NB)

    def gcopy(link, sg, item):
        li = (0 if link == "x" else 2) + (0 if sg > 0 else 1)
        n = SEQ[item]
        color = piece(link, sg, item)
        i = item[1]
        if link == "x":
            row_ = a if item[0] == "p" else wrap(a - sg * item[2], NA)
            at = (row_, x_from(sg, i))
            peer = x_peer(sg)
        else:
            col_ = b if item[0] == "p" else wrap(b - sg * item[2], NB)
            at = (z_from(sg, i), col_)
            peer = z_peer(sg)
        block = full.at[at[0], at[1], core * 4 + color]
        return pltpu.make_async_remote_copy(
            src_ref=block, dst_ref=block, send_sem=g_send.at[li, n], recv_sem=g_recv.at[li, n],
            device_id=peer, device_id_type=MESH,
        )

    waited = set()

    def wait_recv(link, sg, item):
        if (link, sg, item) not in waited:
            waited.add((link, sg, item))
            gcopy(link, sg, item).wait_recv()

    def leads(sg):
        return lo == (1 if sg > 0 else 0)

    core_copies = []

    def core_copy(color, n, block):
        copy = pltpu.make_async_remote_copy(
            src_ref=block, dst_ref=block, send_sem=c_send.at[color, n], recv_sem=c_recv.at[color, n],
            device_id=partner, device_id_type=MESH,
        )
        copy.start()
        core_copies.append(copy)

    def issue(link, sg, item):
        other = "z" if link == "x" else "x"
        i = item[1]
        if item[0] == "r" and item[2] > 0:
            wait_recv(other, sg, ("p", item[2] - 1))
        before = (item[0], i - 1, *item[2:]) if i > 0 else None
        if link == "x":
            if before:
                wait_recv(link, sg, before)
            gcopy(link, sg, item).start()
        else:
            if before:
                wait_recv(link, sg, before)
            first = leads(sg)

            @pl.when(first)
            def _():
                gcopy(link, sg, item).start()

            @pl.when(jnp.logical_not(first))
            def _():
                gcopy(link, sg, item).wait_recv()
                gcopy(link, sg, item).start()

    def wait_recv(link, sg, item):
        if (link, sg, item) in waited:
            return
        waited.add((link, sg, item))
        if link == "x":
            gcopy(link, sg, item).wait_recv()
        else:
            @pl.when(leads(sg))
            def _():
                gcopy(link, sg, item).wait_recv()

    for item in SLOTS:
        for link in ("x", "z"):
            for sg in (1, -1):
                issue(link, sg, item)
        if item == ("r", 0, 3):
            pass

    for link in ("x", "z"):
        for sg in (1, -1):
            for item in SLOTS:
                wait_recv(link, sg, item)
    for sg in (1, -1):
        cx, cz = (0, 2) if sg > 0 else (1, 3)
        for q in range(1, 4):
            core_copy(cx, q - 1, full.at[wrap(a - sg * q, NA), b, core * 4 + cx])
            core_copy(cz, q - 1, full.at[a, wrap(b - sg * q, NB), core * 4 + cz])
        for i in range(3):
            core_copy(cx, 3 + i, full.at[:, wrap(b - sg * (i + 1), NB), core * 4 + cx])
            core_copy(cz, 3 + i, full.at[wrap(a - sg * (i + 1), NA), :, core * 4 + cz])

    @pl.loop(1, NK)
    def _(d):
        a2a(sent, state, in_send, in_recv, d).wait_recv()

    total = jnp.sum(warm_ref[...])
    row16 = lax.broadcasted_iota(jnp.int32, (16, MODES), 0)
    for j in range(NK):
        w = jnp.broadcast_to(warm_ref[j:j + 1, :], (16, MODES))
        hi = w.astype(jnp.bfloat16).astype(jnp.float32)
        mid = (w - hi).astype(jnp.bfloat16).astype(jnp.float32)
        low = w - hi - mid
        parts = jnp.where(row16 == 0, hi, jnp.where(row16 == 1, mid, jnp.where(row16 == 2, low, 0.0)))
        wlhs[:, j * MODES:(j + 1) * MODES] = parts.astype(jnp.bfloat16)

    zi = lax.broadcasted_iota(jnp.int32, (8, 8, MODES), 1)

    def xcopy(t, way):
        return pltpu.make_async_remote_copy(
            src_ref=xs.at[t, way], dst_ref=xr.at[t, way], send_sem=x_send.at[t, way], recv_sem=x_recv.at[t, way],
            device_id=right if way == 0 else left, device_id_type=MESH,
        )

    def zcopy(t, way):
        return pltpu.make_async_remote_copy(
            src_ref=zs.at[t, way], dst_ref=zr.at[t, way], send_sem=z_send.at[t, way], recv_sem=z_recv.at[t, way],
            device_id=z_next if way == 0 else z_prev, device_id_type=MESH,
        )

    for t in range(ITERS):
        xs[t, 0] = state[:, 32:64, :].astype(jnp.bfloat16)
        xcopy(t, 0).start()
        xs[t, 1] = state[:, 0:32, :].astype(jnp.bfloat16)
        xcopy(t, 1).start()
        for j in range(NK):
            zs[t, 0, j] = state[j, pl.ds(7, 8, stride=8), :]
            zs[t, 1, j] = state[j, pl.ds(0, 8, stride=8), :]
        zcopy(t, 0).start()
        zcopy(t, 1).start()
        for way in range(2):
            xcopy(t, way).wait_recv()
            zcopy(t, way).wait_recv()

        def advect(j, energy):
            st = state[j, 0:64, :].reshape(8, 8, MODES)
            cf = [state[j, pl.ds(64 + r, 1), :].reshape(1, 1, MODES) for r in range(6)]
            below = xr[t, 0, j].astype(jnp.float32).reshape(4, 8, MODES)
            above = xr[t, 1, j].astype(jnp.float32).reshape(4, 8, MODES)
            x_below = jnp.concatenate([below, st[0:4]], axis=0)
            x_above = jnp.concatenate([st[4:8], above], axis=0)
            y_below = jnp.concatenate([st[3:4], st[0:3], st[7:8], st[4:7]], axis=0)
            y_above = jnp.concatenate([st[1:4], st[0:1], st[5:8], st[4:5]], axis=0)
            z_lower = zr[t, 0, j].reshape(8, 1, MODES)
            z_upper = zr[t, 1, j].reshape(8, 1, MODES)
            z_below = jnp.where(zi == 0, z_lower, jnp.roll(st, 1, 1))
            z_above = jnp.where(zi == 7, z_upper, jnp.roll(st, -1, 1))
            mv = st
            for d, (lower, upper) in enumerate(((x_below, x_above), (y_below, y_above), (z_below, z_above))):
                mv = mv - (cf[2 * d] * (st - lower) + cf[2 * d + 1] * (st - upper))
            mv = mv.reshape(64, MODES)
            mv_bf = mv.astype(jnp.bfloat16)
            moved[j] = mv
            lhs[:, pl.ds(pl.multiple_of(j * MODES, MODES), MODES)] = mv_bf
            return energy + mv_bf.astype(jnp.float32) * warm_ref[pl.ds(j, 1), :]

        energy = lax.fori_loop(0, NK, advect, jnp.zeros((64, MODES), jnp.float32))
        thermal = jnp.sum(energy, axis=1, keepdims=True) / total
        thermal = jnp.broadcast_to(thermal, (64, MODES))

        if t == 0:
            for copy in core_copies:
                copy.wait_recv()

        nt = (((1,), (1,)), ((), ()))
        target = final if t == ITERS - 1 else state

        @pl.loop(0, NK // 2)
        def _(n):
            w = full[n // 2, pl.ds((n % 2) * 2, 2)].reshape(2 * MODES, M)
            product = lax.dot_general(lhs[...], w, nt, preferred_element_type=jnp.float32)
            if t == 0:
                parts = lax.dot_general(wlhs[...], w, nt, preferred_element_type=jnp.float32)
                both = parts[0:1] + parts[1:2] + parts[2:3]
                relax[2 * n] = jnp.broadcast_to(both[:, :MODES], (8, MODES))
                relax[2 * n + 1] = jnp.broadcast_to(both[:, MODES:], (8, MODES))
            for h in range(2):
                j = 2 * n + h
                pr = product[:, h * MODES:(h + 1) * MODES]
                target[j, 0:64, :] = moved[j] - pr + relax[j, 0:1] * thermal

    lane = lax.broadcasted_iota(jnp.int32, (8, 8, MODES), 2)
    mine = jnp.sum(jnp.where(lane == 8 * k + zi, thermal.reshape(8, 8, MODES), 0.0), axis=1)
    final[:, 64:72, :] = jnp.broadcast_to(mine[None], (NK, 8, MODES))

    @pl.loop(1, NK)
    def _(d):
        a2a(final, landed, o_send, o_recv, d).start()

    landed[k] = final[k]

    @pl.loop(1, NK)
    def _(d):
        a2a(final, landed, o_send, o_recv, d).wait_recv()

    for xy in range(8):
        cells = landed[:, xy * 8:xy * 8 + 8, :].reshape(MODES, MODES)
        out_ref[pl.ds(xy, MODES, stride=8), :] = jnp.transpose(cells)
    therm_ref[...] = jnp.sum(landed[:, 64:72, :], axis=0)

    @pl.loop(1, NK)
    def _(d):
        a2a(sent, state, in_send, in_recv, d).wait_send()
        a2a(final, landed, o_send, o_recv, d).wait_send()

    for link in ("x", "z"):
        for sg in (1, -1):
            for item in SLOTS:
                gcopy(link, sg, item).wait_send()
    for copy in core_copies:
        copy.wait_send()
    for t in range(ITERS):
        for way in range(2):
            xcopy(t, way).wait_send()
            zcopy(t, way).wait_send()


def shards(occupation, offset, warmth, courant, sign, matrix):
    f32, bf16 = jnp.float32, jnp.bfloat16
    dma = pltpu.SemaphoreType.DMA
    vmem = pl.BlockSpec(memory_space=pltpu.VMEM)
    out, therm = pl.pallas_call(
        kernel,
        out_shape=(
            jax.ShapeDtypeStruct((8 * MODES, 128), f32),
            jax.ShapeDtypeStruct((8, 128), f32),
        ),
        in_specs=[vmem] * 5 + [pl.BlockSpec(memory_space=pl.ANY)],
        out_specs=(vmem, vmem),
        scratch_shapes=[
            pltpu.VMEM((NA, NB, 8, 16, M), bf16),
            pltpu.VMEM((NK, 72, MODES), f32),
            pltpu.VMEM((NK, 72, MODES), f32),
            pltpu.VMEM((NK, 72, MODES), f32),
            pltpu.VMEM((NK, 72, MODES), f32),
            pltpu.VMEM((64, M), bf16),
            pltpu.VMEM((16, M), bf16),
            pltpu.VMEM((NK, 8, MODES), f32),
            pltpu.VMEM((ITERS, 2, NK, 32, MODES), bf16),
            pltpu.VMEM((ITERS, 2, NK, 32, MODES), bf16),
            pltpu.VMEM((ITERS, 2, NK, 8, MODES), f32),
            pltpu.VMEM((ITERS, 2, NK, 8, MODES), f32),
            pltpu.VMEM((NK, 64, MODES), f32),
            dma,
            dma((4, 15)), dma((4, 15)),
            dma((4, 6)), dma((4, 6)),
            dma((NK,)), dma((NK,)),
            dma((ITERS, 2)), dma((ITERS, 2)),
            dma((ITERS, 2)), dma((ITERS, 2)),
            dma((NK,)), dma((NK,)),
        ],
        compiler_params=pltpu.CompilerParams(
            collective_id=0, has_side_effects=True, vmem_limit_bytes=48 * 1024 * 1024
        ),
        cost_estimate=pl.CostEstimate(flops=1_700_000_000, bytes_accessed=2_000_000, transcendentals=0),
    )(
        occupation.reshape(8 * MODES, 128),
        offset.reshape(8, 128),
        warmth.reshape(NK, MODES),
        courant,
        sign.reshape(1, MODES),
        matrix.reshape(8, 16, M),
    )
    return out.reshape(occupation.shape), therm.reshape(offset.shape)


def solution(mesh):
    placed = (
        P("mode", "space", None, None),
        P("space", None, None),
        P(),
        P(None, "mode"),
        P("mode"),
        P("mode", None),
    )
    return jax.shard_map(
        shards,
        mesh=mesh,
        in_specs=placed,
        out_specs=(P("mode", "space", None, None), P("space", None, None)),
        check_vma=False,
    )
```

```python
import functools

import jax
import jax.numpy as jnp
from jax import lax
from jax.experimental import pallas as pl
from jax.experimental.pallas import tpu as pltpu
from jax.sharding import PartitionSpec as P

ITERS = 3
NA, NB = 4, 4
NK = NA * NB
NS = 32
MODES = 128
M = NK * MODES
MESH = pl.DeviceIdType.MESH

def kernel(
    occ_ref, t0_ref, warm_ref, cour_ref, sign_ref, s_ref,
    out_ref, therm_ref,
    full, sent, state, final, landed, lhs, wlhs, relax, xs, xr, zs, zr, moved,
    own_sem, gz_send, gz_recv, gx_send, gx_recv, gy_send, gy_recv, c_send, c_recv, in_send, in_recv, x_send, x_recv, z_send, z_recv, o_send, o_recv,
):
    s = lax.axis_index("space")
    k = lax.axis_index("mode")
    a, b = k // NB, k % NB
    lo = s // 16
    core = s % 2

    def dev(space, mode):
        return {"space": space, "mode": mode}

    def wrap(v, n):
        return lax.rem(v + 4 * n, n)

    y = (s // 2) % 8
    toward = 2 * lo - 1
    z_peers = (
        dev(lax.rem(s + 16, NS), wrap(a + toward, NA) * NB + b),
        dev(s, wrap(a + toward, NA) * NB + b),
        dev(lax.rem(s + 16, NS), wrap(a + 2, NA) * NB + b),
    )
    x_up, x_down = dev(s, a * NB + wrap(b + 1, NB)), dev(s, a * NB + wrap(b - 1, NB))
    y_up = dev(lo * 16 + wrap(y + 1, 8) * 2 + core, k)
    y_down = dev(lo * 16 + wrap(y - 1, 8) * 2 + core, k)
    partner = dev(s + 1 - 2 * core, k)
    right, left = dev(wrap(s + 1, NS), k), dev(wrap(s - 1, NS), k)
    z_next, z_prev = dev(s, wrap(k + 1, NK)), dev(s, wrap(k - 1, NK))

    def mode_peer(d):
        return wrap(k + d, NK)

    own = pltpu.make_async_copy(s_ref, full.at[a, b], own_sem)
    own.start()
    barrier = pltpu.get_barrier_semaphore()

    @pl.loop(1, NK)
    def _(d):
        pl.semaphore_signal(barrier, inc=1, device_id=dev(s, mode_peer(d)), device_id_type=MESH)

    for peer in (right, left, z_peers[0], z_peers[2], y_up, y_down):
        pl.semaphore_signal(barrier, inc=1, device_id=peer, device_id_type=MESH)

    warm_col = jnp.transpose(jnp.broadcast_to(warm_ref[pl.ds(k, 1), :], (MODES, MODES)))
    for xy in range(8):
        cells = occ_ref[pl.ds(xy, MODES, stride=8), :] + warm_col * t0_ref[xy:xy + 1, :]
        sent[:, pl.ds(xy * 8, 8), :] = jnp.transpose(cells).reshape(NK, 8, MODES)
    sign = sign_ref[...]
    row = lax.broadcasted_iota(jnp.int32, (8, MODES), 0)
    coef = jnp.zeros((8, MODES), jnp.float32)
    for d in range(3):
        bit = jnp.broadcast_to((sign >> d) & 1, (8, MODES))
        c = jnp.broadcast_to(cour_ref[d:d + 1, :], (8, MODES))
        coef = jnp.where(row == 2 * d, jnp.where(bit == 0, c, 0.0), coef)
        coef = jnp.where(row == 2 * d + 1, jnp.where(bit == 1, c, 0.0), coef)
    sent[:, 64:72, :] = jnp.broadcast_to(coef[None], (NK, 8, MODES))

    pl.semaphore_wait(barrier, NK - 1 + 6)

    def a2a(src, dst, send, recv, d):
        there = mode_peer(d)
        return pltpu.make_async_remote_copy(
            src_ref=src.at[there], dst_ref=dst.at[k], send_sem=send.at[d], recv_sem=recv.at[d],
            device_id=dev(s, there), device_id_type=MESH,
        )

    own.wait()
    rows = [a, wrap(a + toward, NA), wrap(a - toward, NA), wrap(a + 2, NA)]
    cols = [b, wrap(b - 1, NB), wrap(b + 1, NB), wrap(b + 2, NB)]
    mine_u = (y % 2) * 4 + core * 2
    other_u = (1 - y % 2) * 4 + core * 2
    started = []

    def remote(block, send, recv, peer):
        return pltpu.make_async_remote_copy(
            src_ref=block, dst_ref=block, send_sem=send, recv_sem=recv, device_id=peer, device_id_type=MESH
        )

    def z_copy(n):
        return remote(full.at[a, b, pl.ds(mine_u, 2)], gz_send.at[n], gz_recv.at[n], z_peers[n - 1])

    def x_copy(n, step):
        if step < 2:
            block = full.at[rows[n], b, pl.ds(mine_u, 2)]
        else:
            block = full.at[rows[n], cols[step - 1], mine_u + step - 2]
        return remote(block, gx_send.at[n, step], gx_recv.at[n, step], x_down if step % 2 else x_up)

    def y_copy(n, m, way):
        block = full.at[rows[n], cols[m], mine_u + way]
        return remote(block, gy_send.at[n, m, way], gy_recv.at[n, m, way], y_down if way else y_up)

    def core_copy(n, m, kind):
        block = full.at[rows[n], cols[m], pl.ds(other_u if kind else mine_u, 2)]
        return remote(block, c_send.at[n, m, kind], c_recv.at[n, m, kind], partner)

    def start(copy):
        copy.start()
        started.append(copy)

    def share(n, m):
        start(y_copy(n, m, 0))
        start(y_copy(n, m, 1))
        start(core_copy(n, m, 0))

    for n in range(1, 4):
        start(z_copy(n))
    start(x_copy(0, 0))
    start(x_copy(0, 1))

    @pl.loop(1, NK)
    def _(d):
        a2a(sent, state, in_send, in_recv, d).start()

    state[k] = sent[k]

    for n in range(7):
        if 0 < n < 4:
            z_copy(n).wait_recv()
            start(x_copy(n, 0))
            start(x_copy(n, 1))
            share(n, 0)
        if 0 <= n - 1 < 4:
            for m in (1, 2):
                x_copy(n - 1, m - 1).wait_recv()
                start(x_copy(n - 1, m + 1))
            share(n - 1, 1)
            share(n - 1, 2)
        if 0 <= n - 2 < 4:
            x_copy(n - 2, 2).wait_recv()
            x_copy(n - 2, 3).wait_recv()
            share(n - 2, 3)
        if 0 <= n - 3 < 4:
            for m in range(4):
                if n - 3 or m:
                    y_copy(n - 3, m, 0).wait_recv()
                    y_copy(n - 3, m, 1).wait_recv()
                    start(core_copy(n - 3, m, 1))

    @pl.loop(1, NK)
    def _(d):
        a2a(sent, state, in_send, in_recv, d).wait_recv()

    total = jnp.sum(warm_ref[...])
    row16 = lax.broadcasted_iota(jnp.int32, (16, MODES), 0)
    for j in range(NK):
        w = jnp.broadcast_to(warm_ref[j:j + 1, :], (16, MODES))
        hi = w.astype(jnp.bfloat16).astype(jnp.float32)
        mid = (w - hi).astype(jnp.bfloat16).astype(jnp.float32)
        low = w - hi - mid
        parts = jnp.where(row16 == 0, hi, jnp.where(row16 == 1, mid, jnp.where(row16 == 2, low, 0.0)))
        wlhs[:, j * MODES:(j + 1) * MODES] = parts.astype(jnp.bfloat16)

    zi = lax.broadcasted_iota(jnp.int32, (8, 8, MODES), 1)

    def xcopy(t, way):
        return pltpu.make_async_remote_copy(
            src_ref=xs.at[t, way], dst_ref=xr.at[t, way], send_sem=x_send.at[t, way], recv_sem=x_recv.at[t, way],
            device_id=right if way == 0 else left, device_id_type=MESH,
        )

    def zcopy(t, way):
        return pltpu.make_async_remote_copy(
            src_ref=zs.at[t, way], dst_ref=zr.at[t, way], send_sem=z_send.at[t, way], recv_sem=z_recv.at[t, way],
            device_id=z_next if way == 0 else z_prev, device_id_type=MESH,
        )

    for t in range(ITERS):
        xs[t, 0] = state[:, 32:64, :].astype(jnp.bfloat16)
        xcopy(t, 0).start()
        xs[t, 1] = state[:, 0:32, :].astype(jnp.bfloat16)
        xcopy(t, 1).start()
        for j in range(NK):
            zs[t, 0, j] = state[j, pl.ds(7, 8, stride=8), :]
            zs[t, 1, j] = state[j, pl.ds(0, 8, stride=8), :]
        zcopy(t, 0).start()
        zcopy(t, 1).start()
        for way in range(2):
            xcopy(t, way).wait_recv()
            zcopy(t, way).wait_recv()

        def advect(j, energy):
            st = state[j, 0:64, :].reshape(8, 8, MODES)
            cf = [state[j, pl.ds(64 + r, 1), :].reshape(1, 1, MODES) for r in range(6)]
            below = xr[t, 0, j].astype(jnp.float32).reshape(4, 8, MODES)
            above = xr[t, 1, j].astype(jnp.float32).reshape(4, 8, MODES)
            x_below = jnp.concatenate([below, st[0:4]], axis=0)
            x_above = jnp.concatenate([st[4:8], above], axis=0)
            y_below = jnp.concatenate([st[3:4], st[0:3], st[7:8], st[4:7]], axis=0)
            y_above = jnp.concatenate([st[1:4], st[0:1], st[5:8], st[4:5]], axis=0)
            z_lower = zr[t, 0, j].reshape(8, 1, MODES)
            z_upper = zr[t, 1, j].reshape(8, 1, MODES)
            z_below = jnp.where(zi == 0, z_lower, jnp.roll(st, 1, 1))
            z_above = jnp.where(zi == 7, z_upper, jnp.roll(st, -1, 1))
            mv = st
            for d, (lower, upper) in enumerate(((x_below, x_above), (y_below, y_above), (z_below, z_above))):
                mv = mv - (cf[2 * d] * (st - lower) + cf[2 * d + 1] * (st - upper))
            mv = mv.reshape(64, MODES)
            mv_bf = mv.astype(jnp.bfloat16)
            moved[j] = mv
            lhs[:, pl.ds(pl.multiple_of(j * MODES, MODES), MODES)] = mv_bf
            return energy + mv_bf.astype(jnp.float32) * warm_ref[pl.ds(j, 1), :]

        energy = lax.fori_loop(0, NK, advect, jnp.zeros((64, MODES), jnp.float32))
        thermal = jnp.sum(energy, axis=1, keepdims=True) / total
        thermal = jnp.broadcast_to(thermal, (64, MODES))

        if t == 0:
            for n in range(4):
                for m in range(4):
                    if n or m:
                        core_copy(n, m, 0).wait_recv()
                        core_copy(n, m, 1).wait_recv()

        nt = (((1,), (1,)), ((), ()))
        last = t == ITERS - 1
        target = final if last else state
        if last:
            lane = lax.broadcasted_iota(jnp.int32, (8, 8, MODES), 2)
            mine = jnp.sum(jnp.where(lane == 8 * k + zi, thermal.reshape(8, 8, MODES), 0.0), axis=1)
            final[:, 64:72, :] = jnp.broadcast_to(mine[None], (NK, 8, MODES))

        @pl.loop(0, NK // 2)
        def _(step):
            n = lax.rem(k // 2 + step, NK // 2)
            w = full[n // 2, pl.ds((n % 2) * 2, 2)].reshape(2 * MODES, M)
            product = lax.dot_general(lhs[...], w, nt, preferred_element_type=jnp.float32)
            if t == 0:
                parts = lax.dot_general(wlhs[...], w, nt, preferred_element_type=jnp.float32)
                both = parts[0:1] + parts[1:2] + parts[2:3]
                relax[2 * n] = jnp.broadcast_to(both[:, :MODES], (8, MODES))
                relax[2 * n + 1] = jnp.broadcast_to(both[:, MODES:], (8, MODES))
            for h in range(2):
                j = 2 * n + h
                pr = product[:, h * MODES:(h + 1) * MODES]
                target[j, 0:64, :] = moved[j] - pr + relax[j, 0:1] * thermal
                if last:
                    d = lax.rem(j - k + NK, NK)

                    @pl.when(d > 0)
                    def _():
                        a2a(final, landed, o_send, o_recv, d).start()

    landed[k] = final[k]

    @pl.loop(1, NK)
    def _(d):
        a2a(final, landed, o_send, o_recv, d).wait_recv()

    for xy in range(8):
        cells = landed[:, xy * 8:xy * 8 + 8, :].reshape(MODES, MODES)
        out_ref[pl.ds(xy, MODES, stride=8), :] = jnp.transpose(cells)
    therm_ref[...] = jnp.sum(landed[:, 64:72, :], axis=0)

    @pl.loop(1, NK)
    def _(d):
        a2a(sent, state, in_send, in_recv, d).wait_send()
        a2a(final, landed, o_send, o_recv, d).wait_send()

    for copy in started:
        copy.wait_send()
    for t in range(ITERS):
        for way in range(2):
            xcopy(t, way).wait_send()
            zcopy(t, way).wait_send()


def shards(occupation, offset, warmth, courant, sign, matrix):
    f32, bf16 = jnp.float32, jnp.bfloat16
    dma = pltpu.SemaphoreType.DMA
    vmem = pl.BlockSpec(memory_space=pltpu.VMEM)
    out, therm = pl.pallas_call(
        kernel,
        out_shape=(
            jax.ShapeDtypeStruct((8 * MODES, 128), f32),
            jax.ShapeDtypeStruct((8, 128), f32),
        ),
        in_specs=[vmem] * 5 + [pl.BlockSpec(memory_space=pl.ANY)],
        out_specs=(vmem, vmem),
        scratch_shapes=[
            pltpu.VMEM((NA, NB, 8, 16, M), bf16),
            pltpu.VMEM((NK, 72, MODES), f32),
            pltpu.VMEM((NK, 72, MODES), f32),
            pltpu.VMEM((NK, 72, MODES), f32),
            pltpu.VMEM((NK, 72, MODES), f32),
            pltpu.VMEM((64, M), bf16),
            pltpu.VMEM((16, M), bf16),
            pltpu.VMEM((NK, 8, MODES), f32),
            pltpu.VMEM((ITERS, 2, NK, 32, MODES), bf16),
            pltpu.VMEM((ITERS, 2, NK, 32, MODES), bf16),
            pltpu.VMEM((ITERS, 2, NK, 8, MODES), f32),
            pltpu.VMEM((ITERS, 2, NK, 8, MODES), f32),
            pltpu.VMEM((NK, 64, MODES), f32),
            dma,
            dma((4,)), dma((4,)),
            dma((4, 4)), dma((4, 4)),
            dma((4, 4, 2)), dma((4, 4, 2)),
            dma((4, 4, 2)), dma((4, 4, 2)),
            dma((NK,)), dma((NK,)),
            dma((ITERS, 2)), dma((ITERS, 2)),
            dma((ITERS, 2)), dma((ITERS, 2)),
            dma((NK,)), dma((NK,)),
        ],
        compiler_params=pltpu.CompilerParams(
            collective_id=0, has_side_effects=True, vmem_limit_bytes=48 * 1024 * 1024
        ),
        cost_estimate=pl.CostEstimate(flops=1_700_000_000, bytes_accessed=2_000_000, transcendentals=0),
    )(
        occupation.reshape(8 * MODES, 128),
        offset.reshape(8, 128),
        warmth.reshape(NK, MODES),
        courant,
        sign.reshape(1, MODES),
        matrix.reshape(8, 16, M),
    )
    return out.reshape(occupation.shape), therm.reshape(offset.shape)


def solution(mesh):
    placed = (
        P("mode", "space", None, None),
        P("space", None, None),
        P(),
        P(None, "mode"),
        P("mode"),
        P("mode", None),
    )
    return jax.shard_map(
        shards,
        mesh=mesh,
        in_specs=placed,
        out_specs=(P("mode", "space", None, None), P("space", None, None)),
        check_vma=False,
    )
```

```python
import functools

import jax
import jax.numpy as jnp
from jax import lax
from jax.experimental import pallas as pl
from jax.experimental.pallas import tpu as pltpu
from jax.sharding import PartitionSpec as P

ITERS = 3
NA, NB = 4, 4
NK = NA * NB
NS = 32
MODES = 128
M = NK * MODES
MESH = pl.DeviceIdType.MESH

def kernel(
    occ_hbm, t0_hbm, warm_hbm, cour_hbm, sign_hbm, s_hbm,
    out_ref, therm_ref,
    occ_ref, t0_ref, warm_ref, cour_ref, sign_ref,
    full, sent, state, q_sent, q_state, coef_sent, coefs, q_final, q_landed, tail, tails, back, lhs, wlhs, relax, xs, xr, zs, zr, moved, half,
    fetch_sem, own_sem, gz_send, gz_recv, gx_send, gx_recv, gy_send, gy_recv, c_send, c_recv, in_send, in_recv, x_send, x_recv, z_send, z_recv, o_send, o_recv,
):
    s = lax.axis_index("space")
    k = lax.axis_index("mode")
    a, b = k // NB, k % NB
    lo = s // 16
    core = s % 2

    def dev(space, mode):
        return {"space": space, "mode": mode}

    def wrap(v, n):
        return lax.rem(v + 4 * n, n)

    y = (s // 2) % 8
    toward = 2 * lo - 1
    z_peers = (
        dev(lax.rem(s + 16, NS), wrap(a + toward, NA) * NB + b),
        dev(s, wrap(a + toward, NA) * NB + b),
        dev(lax.rem(s + 16, NS), wrap(a + 2, NA) * NB + b),
    )
    x_up, x_down = dev(s, a * NB + wrap(b + 1, NB)), dev(s, a * NB + wrap(b - 1, NB))
    y_up = dev(lo * 16 + wrap(y + 1, 8) * 2 + core, k)
    y_down = dev(lo * 16 + wrap(y - 1, 8) * 2 + core, k)
    partner = dev(s + 1 - 2 * core, k)
    right, left = dev(wrap(s + 1, NS), k), dev(wrap(s - 1, NS), k)
    z_next, z_prev = dev(s, wrap(k + 1, NK)), dev(s, wrap(k - 1, NK))

    def mode_peer(d):
        return wrap(k + d, NK)

    fetches = [
        pltpu.make_async_copy(src, dst, fetch_sem.at[i])
        for i, (src, dst) in enumerate((
            (occ_hbm, occ_ref), (t0_hbm, t0_ref), (warm_hbm, warm_ref), (cour_hbm, cour_ref), (sign_hbm, sign_ref),
        ))
    ]
    for fetch in fetches:
        fetch.start()
    own = pltpu.make_async_copy(s_hbm, full.at[a, b], own_sem)
    own.start()
    barrier = pltpu.get_barrier_semaphore()

    @pl.loop(1, NK)
    def _(d):
        pl.semaphore_signal(barrier, inc=1, device_id=dev(s, mode_peer(d)), device_id_type=MESH)

    for peer in (right, left, z_peers[0], z_peers[2], y_up, y_down):
        pl.semaphore_signal(barrier, inc=1, device_id=peer, device_id_type=MESH)

    pl.semaphore_wait(barrier, NK - 1 + 6)

    own.wait()
    rows = [a, wrap(a + toward, NA), wrap(a - toward, NA), wrap(a + 2, NA)]
    cols = [b, wrap(b - 1, NB), wrap(b + 1, NB), wrap(b + 2, NB)]
    mine_u = (y % 2) * 4 + core * 2
    other_u = (1 - y % 2) * 4 + core * 2
    started = []

    def remote(block, send, recv, peer):
        return pltpu.make_async_remote_copy(
            src_ref=block, dst_ref=block, send_sem=send, recv_sem=recv, device_id=peer, device_id_type=MESH
        )

    def z_copy(n, kind):
        block = full.at[a, b, pl.ds(other_u if kind else mine_u, 2)]
        return remote(block, gz_send.at[n, kind], gz_recv.at[n, kind], z_peers[n - 1])

    def x_copy(n, step, kind=0):
        if step < 2:
            block = full.at[rows[n], b, pl.ds(other_u if kind else mine_u, 2)]
        else:
            block = full.at[rows[n], cols[step - 1], mine_u + step - 2]
        return remote(block, gx_send.at[n, step, kind], gx_recv.at[n, step, kind], x_down if step % 2 else x_up)

    def y_copy(n, m, way):
        block = full.at[rows[n], cols[m], mine_u + way]
        return remote(block, gy_send.at[n, m, way], gy_recv.at[n, m, way], y_down if way else y_up)

    def core_copy(n, m, kind):
        block = full.at[rows[n], cols[m], pl.ds(other_u if kind else mine_u, 2)]
        return remote(block, c_send.at[n, m, kind], c_recv.at[n, m, kind], partner)

    def start(copy):
        copy.start()
        started.append(copy)

    def whole(n, m):
        return (n, m) in ((0, 0), (0, 1), (0, 2), (1, 0))

    def share(n, m):
        if not whole(n, m):
            start(y_copy(n, m, 0))
            start(y_copy(n, m, 1))
        start(core_copy(n, m, 0))

    start(z_copy(1, 0))
    start(x_copy(0, 0))
    start(x_copy(0, 1))
    start(z_copy(2, 0))
    start(z_copy(3, 0))
    start(x_copy(0, 0, 1))
    start(x_copy(0, 1, 1))
    start(z_copy(1, 1))

    def a2a(src, dst, extra, extra_dst, send, recv, d):
        there = mode_peer(d)
        return [
            pltpu.make_async_remote_copy(
                src_ref=s_.at[there], dst_ref=d_.at[k], send_sem=send.at[d, i], recv_sem=recv.at[d, i],
                device_id=dev(s, there), device_id_type=MESH,
            )
            for i, (s_, d_) in enumerate(((src, dst), (extra, extra_dst)))
        ]

    def a2a_in(d):
        return a2a(q_sent, q_state, coef_sent, coefs, in_send, in_recv, d)

    def a2a_out(d):
        return a2a(q_final, q_landed, tail, tails, o_send, o_recv, d)

    def quantized(values):
        most = jnp.max(jnp.abs(values), axis=0, keepdims=True)
        steps = jnp.where(most > 0.0, 32767.0 / most, 0.0)
        return jnp.round(values * steps).astype(jnp.int32).astype(jnp.int16), most * (1.0 / 32767.0)

    def restored(q, step):
        return q.astype(jnp.int32).astype(jnp.float32) * step

    for fetch in fetches:
        fetch.wait()

    warm_col = jnp.transpose(jnp.broadcast_to(warm_ref[pl.ds(k, 1), :], (MODES, MODES)))
    for xy in range(8):
        cells = occ_ref[pl.ds(xy, MODES, stride=8), :] + warm_col * t0_ref[xy:xy + 1, :]
        sent[:, pl.ds(xy * 8, 8), :] = jnp.transpose(cells).reshape(NK, 8, MODES)
    sign = sign_ref[...]
    row = lax.broadcasted_iota(jnp.int32, (8, MODES), 0)
    coef = jnp.zeros((8, MODES), jnp.float32)
    for d in range(3):
        bit = jnp.broadcast_to((sign >> d) & 1, (8, MODES))
        c = jnp.broadcast_to(cour_ref[d:d + 1, :], (8, MODES))
        coef = jnp.where(row == 2 * d, jnp.where(bit == 0, c, 0.0), coef)
        coef = jnp.where(row == 2 * d + 1, jnp.where(bit == 1, c, 0.0), coef)

    @pl.loop(0, NK)
    def _(j):
        q, step = quantized(sent[j])
        q_sent[j] = q
        coef_sent[j] = jnp.where(row == 6, jnp.broadcast_to(step, (8, MODES)), coef)

    @pl.loop(1, NK)
    def _(d):
        for copy in a2a_in(d):
            copy.start()

    q_state[k] = q_sent[k]
    coefs[k] = coef_sent[k]

    def gather_stage(n):
        if 0 < n < 4:
            z_copy(n, 0).wait_recv()
            start(x_copy(n, 0))
            start(x_copy(n, 1))
            share(n, 0)
        if 0 <= n - 1 < 4:
            for m in (1, 2):
                x_copy(n - 1, m - 1).wait_recv()
                start(x_copy(n - 1, m + 1))
            share(n - 1, 1)
            share(n - 1, 2)
        if 0 <= n - 2 < 4:
            x_copy(n - 2, 2).wait_recv()
            x_copy(n - 2, 3).wait_recv()
            share(n - 2, 3)
        if 0 <= n - 3 < 4:
            for m in range(4):
                if n - 3 or m:
                    if not whole(n - 3, m):
                        y_copy(n - 3, m, 0).wait_recv()
                        y_copy(n - 3, m, 1).wait_recv()
                    elif m:
                        x_copy(0, m - 1, 1).wait_recv()
                    else:
                        z_copy(1, 1).wait_recv()
                    start(core_copy(n - 3, m, 1))

    for n in range(4):
        gather_stage(n)

    total = jnp.sum(warm_ref[...])
    zi = lax.broadcasted_iota(jnp.int32, (8, 8, MODES), 1)
    nt = (((1,), (1,)), ((), ()))
    H = NK // 2

    def halo_copies(t, h):
        part = pl.ds(h * H, H)
        return [
            pltpu.make_async_remote_copy(
                src_ref=src.at[t, way, part], dst_ref=dst.at[t, way, part],
                send_sem=send.at[t, way, h], recv_sem=recv.at[t, way, h], device_id=peer, device_id_type=MESH,
            )
            for src, dst, send, recv, peers in (
                (xs, xr, x_send, x_recv, (right, left)), (zs, zr, z_send, z_recv, (z_next, z_prev)),
            )
            for way, peer in enumerate(peers)
        ]

    def stage_halo(t, j):
        xs[t, 0, j] = state[j, 32:64, :].astype(jnp.bfloat16)
        xs[t, 1, j] = state[j, 0:32, :].astype(jnp.bfloat16)
        zs[t, 0, j] = state[j, pl.ds(7, 8, stride=8), :]
        zs[t, 1, j] = state[j, pl.ds(0, 8, stride=8), :]

    def send_halo(t, h):
        for copy in halo_copies(t, h):
            copy.start()

    def advect_block(t, j, energy):
        st = state[j].reshape(8, 8, MODES)
        cf = [coefs[j, pl.ds(r, 1), :].reshape(1, 1, MODES) for r in range(6)]
        below = xr[t, 0, j].astype(jnp.float32).reshape(4, 8, MODES)
        above = xr[t, 1, j].astype(jnp.float32).reshape(4, 8, MODES)
        x_below = jnp.concatenate([below, st[0:4]], axis=0)
        x_above = jnp.concatenate([st[4:8], above], axis=0)
        y_below = jnp.concatenate([st[3:4], st[0:3], st[7:8], st[4:7]], axis=0)
        y_above = jnp.concatenate([st[1:4], st[0:1], st[5:8], st[4:5]], axis=0)
        z_lower = zr[t, 0, j].reshape(8, 1, MODES)
        z_upper = zr[t, 1, j].reshape(8, 1, MODES)
        z_below = jnp.where(zi == 0, z_lower, jnp.roll(st, 1, 1))
        z_above = jnp.where(zi == 7, z_upper, jnp.roll(st, -1, 1))
        mv = st
        for d, (lower, upper) in enumerate(((x_below, x_above), (y_below, y_above), (z_below, z_above))):
            mv = mv - (cf[2 * d] * (st - lower) + cf[2 * d + 1] * (st - upper))
        mv = mv.reshape(64, MODES)
        mv_bf = mv.astype(jnp.bfloat16)
        moved[j] = mv
        lhs[:, pl.ds(pl.multiple_of(j * MODES, MODES), MODES)] = mv_bf
        return energy + mv_bf.astype(jnp.float32) * warm_ref[pl.ds(j, 1), :]

    def advect(t, h, energy):
        for copy in halo_copies(t, h):
            copy.wait_recv()
        return lax.fori_loop(h * H, h * H + H, functools.partial(advect_block, t), energy)

    def offset(energy):
        thermal = jnp.sum(energy, axis=1, keepdims=True) / total
        return jnp.broadcast_to(thermal, (64, MODES))

    nothing = jnp.zeros((64, MODES), jnp.float32)

    row16 = lax.broadcasted_iota(jnp.int32, (16, MODES), 0)
    for j in range(NK):
        w = jnp.broadcast_to(warm_ref[j:j + 1, :], (16, MODES))
        hi = w.astype(jnp.bfloat16).astype(jnp.float32)
        mid = (w - hi).astype(jnp.bfloat16).astype(jnp.float32)
        low = w - hi - mid
        parts = jnp.where(row16 == 0, hi, jnp.where(row16 == 1, mid, jnp.where(row16 == 2, low, 0.0)))
        wlhs[:, j * MODES:(j + 1) * MODES] = parts.astype(jnp.bfloat16)

    @pl.loop(1, NK)
    def _(d):
        for copy in a2a_in(d):
            copy.wait_recv()

    for h in range(2):
        @pl.loop(h * H, h * H + H)
        def _(j):
            state[j] = restored(q_state[j], coefs[j, 6:7])
            stage_halo(0, j)

        send_halo(0, h)

    gather_stage(4)
    gather_stage(5)
    thermal = offset(advect(0, 1, advect(0, 0, nothing)))
    gather_stage(6)

    for n in range(4):
        for m in range(4):
            if n or m:
                core_copy(n, m, 0).wait_recv()
                core_copy(n, m, 1).wait_recv()

        @pl.loop(0, 2)
        def _(pair):
            r = rows[n]
            w = full[r, pl.ds(pair * 2, 2)].reshape(2 * MODES, M)
            product = lax.dot_general(lhs[...], w, nt, preferred_element_type=jnp.float32)
            parts = lax.dot_general(wlhs[...], w, nt, preferred_element_type=jnp.float32)
            both = parts[0:1] + parts[1:2] + parts[2:3]
            for e in range(2):
                j = r * NB + pair * 2 + e
                rx = jnp.broadcast_to(both[:, e * MODES:(e + 1) * MODES], (8, MODES))
                relax[j] = rx
                state[j] = moved[j] - product[:, e * MODES:(e + 1) * MODES] + rx[0:1] * thermal
                stage_halo(1, j)

    for h in range(2):
        send_halo(1, h)

    for t in range(1, ITERS):
        last = t == ITERS - 1
        energy = advect(t, 0, nothing)

        @pl.loop(0, H)
        def _(n):
            w = full[n // 2, pl.ds((n % 2) * 2, 2), :, :, 0:M // 2].reshape(2 * MODES, M // 2)
            half[n] = lax.dot_general(lhs[:, 0:M // 2], w, nt, preferred_element_type=jnp.float32)

        thermal = offset(advect(t, 1, energy))
        if last:
            lane = lax.broadcasted_iota(jnp.int32, (8, 8, MODES), 2)
            mine = jnp.sum(jnp.where(lane == 8 * k + zi, thermal.reshape(8, 8, MODES), 0.0), axis=1)
            tail[:, 0:8, :] = jnp.broadcast_to(mine[None], (NK, 8, MODES))

        def finish(n):
            w = full[n // 2, pl.ds((n % 2) * 2, 2), :, :, M // 2:M].reshape(2 * MODES, M // 2)
            product = half[n] + lax.dot_general(lhs[:, M // 2:M], w, nt, preferred_element_type=jnp.float32)
            for e in range(2):
                j = 2 * n + e
                new = moved[j] - product[:, e * MODES:(e + 1) * MODES] + relax[j, 0:1] * thermal
                if last:
                    q, step = quantized(new)
                    q_final[j] = q
                    tail[j, 8:16, :] = jnp.broadcast_to(step, (8, MODES))
                    d = lax.rem(j - k + NK, NK)

                    @pl.when(d > 0)
                    def _():
                        for copy in a2a_out(d):
                            copy.start()
                else:
                    state[j] = new
                    stage_halo(t + 1, j)

        if last:
            @pl.loop(0, H)
            def _(step):
                finish(lax.rem(k // 2 + step, H))
        else:
            for h in range(2):
                @pl.loop(h * H // 2, (h + 1) * H // 2)
                def _(n):
                    finish(n)

                send_halo(t + 1, h)

    q_landed[k] = q_final[k]
    tails[k] = tail[k]

    @pl.loop(1, NK)
    def _(d):
        for copy in a2a_out(d):
            copy.wait_recv()

    @pl.loop(0, NK)
    def _(j):
        back[j] = restored(q_landed[j], tails[j, 8:9]).reshape(8, 8, MODES)

    for xy in range(8):
        cells = back[:, xy].reshape(MODES, MODES)
        out_ref[pl.ds(xy, MODES, stride=8), :] = jnp.transpose(cells)
    therm_ref[...] = jnp.sum(tails[:, 0:8, :], axis=0)

    @pl.loop(1, NK)
    def _(d):
        for copy in a2a_in(d) + a2a_out(d):
            copy.wait_send()

    for copy in started:
        copy.wait_send()
    for t in range(ITERS):
        for h in range(2):
            for copy in halo_copies(t, h):
                copy.wait_send()


def shards(occupation, offset, warmth, courant, sign, matrix):
    f32, bf16 = jnp.float32, jnp.bfloat16
    dma = pltpu.SemaphoreType.DMA
    vmem = pl.BlockSpec(memory_space=pltpu.VMEM)
    out, therm = pl.pallas_call(
        kernel,
        out_shape=(
            jax.ShapeDtypeStruct((8 * MODES, 128), f32),
            jax.ShapeDtypeStruct((8, 128), f32),
        ),
        in_specs=[pl.BlockSpec(memory_space=pltpu.HBM)] * 6,
        out_specs=(vmem, vmem),
        scratch_shapes=[
            pltpu.VMEM((8 * MODES, 128), f32),
            pltpu.VMEM((8, 128), f32),
            pltpu.VMEM((NK, MODES), f32),
            pltpu.VMEM((3, MODES), f32),
            pltpu.VMEM((1, MODES), jnp.int32),
            pltpu.VMEM((NA, NB, 8, 16, M), bf16),
            pltpu.VMEM((NK, 64, MODES), f32),
            pltpu.VMEM((NK, 64, MODES), f32),
            pltpu.VMEM((NK, 64, MODES), jnp.int16),
            pltpu.VMEM((NK, 64, MODES), jnp.int16),
            pltpu.VMEM((NK, 8, MODES), f32),
            pltpu.VMEM((NK, 8, MODES), f32),
            pltpu.VMEM((NK, 64, MODES), jnp.int16),
            pltpu.VMEM((NK, 64, MODES), jnp.int16),
            pltpu.VMEM((NK, 16, MODES), f32),
            pltpu.VMEM((NK, 16, MODES), f32),
            pltpu.VMEM((NK, 8, 8, MODES), f32),
            pltpu.VMEM((64, M), bf16),
            pltpu.VMEM((16, M), bf16),
            pltpu.VMEM((NK, 8, MODES), f32),
            pltpu.VMEM((ITERS, 2, NK, 32, MODES), bf16),
            pltpu.VMEM((ITERS, 2, NK, 32, MODES), bf16),
            pltpu.VMEM((ITERS, 2, NK, 8, MODES), f32),
            pltpu.VMEM((ITERS, 2, NK, 8, MODES), f32),
            pltpu.VMEM((NK, 64, MODES), f32),
            pltpu.VMEM((NK // 2, 64, 2 * MODES), f32),
            dma((5,)),
            dma,
            dma((4, 2)), dma((4, 2)),
            dma((4, 4, 2)), dma((4, 4, 2)),
            dma((4, 4, 2)), dma((4, 4, 2)),
            dma((4, 4, 2)), dma((4, 4, 2)),
            dma((NK, 2)), dma((NK, 2)),
            dma((ITERS, 2, 2)), dma((ITERS, 2, 2)),
            dma((ITERS, 2, 2)), dma((ITERS, 2, 2)),
            dma((NK, 2)), dma((NK, 2)),
        ],
        compiler_params=pltpu.CompilerParams(
            collective_id=0, has_side_effects=True, vmem_limit_bytes=62 * 1024 * 1024
        ),
        cost_estimate=pl.CostEstimate(flops=1_700_000_000, bytes_accessed=2_000_000, transcendentals=0),
    )(
        occupation.reshape(8 * MODES, 128),
        offset.reshape(8, 128),
        warmth.reshape(NK, MODES),
        courant,
        sign.reshape(1, MODES),
        matrix.reshape(8, 16, M),
    )
    return out.reshape(occupation.shape), therm.reshape(offset.shape)


def solution(mesh):
    placed = (
        P("mode", "space", None, None),
        P("space", None, None),
        P(),
        P(None, "mode"),
        P("mode"),
        P("mode", None),
    )
    return jax.shard_map(
        shards,
        mesh=mesh,
        in_specs=placed,
        out_specs=(P("mode", "space", None, None), P("space", None, None)),
        check_vma=False,
    )
```

```python
import functools

import jax
import jax.numpy as jnp
from jax import lax
from jax.experimental import pallas as pl
from jax.experimental.pallas import tpu as pltpu
from jax.sharding import PartitionSpec as P

ITERS = 3
NA, NB = 4, 4
NK = NA * NB
NS = 32
MODES = 128
M = NK * MODES
MESH = pl.DeviceIdType.MESH

def kernel(
    occ_hbm, t0_hbm, warm_hbm, cour_hbm, sign_hbm, s_hbm,
    q_landed, tails,
    occ_ref, t0_ref, warm_ref, cour_ref, sign_ref,
    full, sent, state, q_sent, q_state, coef_sent, coefs, q_final, tail, lhs, wlhs, relax, xs, xr, zs, zr, moved, half,
    fetch_sem, kept_sem, own_sem, gz_send, gz_recv, gx_send, gx_recv, gy_send, gy_recv, gp_send, gp_recv, c_send, c_recv, in_send, in_recv, x_send, x_recv, z_send, z_recv, o_send, o_recv,
):
    s = lax.axis_index("space")
    k = lax.axis_index("mode")
    a, b = k // NB, k % NB
    lo = s // 16
    core = s % 2

    def dev(space, mode):
        return {"space": space, "mode": mode}

    def wrap(v, n):
        return lax.rem(v + 4 * n, n)

    y = (s // 2) % 8
    toward = 2 * lo - 1
    z_peers = (
        dev(lax.rem(s + 16, NS), wrap(a + toward, NA) * NB + b),
        dev(s, wrap(a + toward, NA) * NB + b),
        dev(lax.rem(s + 16, NS), wrap(a + 2, NA) * NB + b),
    )
    x_up, x_down = dev(s, a * NB + wrap(b + 1, NB)), dev(s, a * NB + wrap(b - 1, NB))
    z_pair = dev(lax.rem(s + 16, NS), k)
    y_up = dev(lo * 16 + wrap(y + 1, 8) * 2 + core, k)
    y_down = dev(lo * 16 + wrap(y - 1, 8) * 2 + core, k)
    partner = dev(s + 1 - 2 * core, k)
    right, left = dev(wrap(s + 1, NS), k), dev(wrap(s - 1, NS), k)

    def block_of(mode):
        aa, bb = mode // NB, mode % NB
        return aa * NB + bb + (aa % 2) * (NB - 1 - 2 * bb)

    zb = block_of(k)
    z_next, z_prev = dev(s, block_of(wrap(zb + 1, NK))), dev(s, block_of(wrap(zb - 1, NK)))

    def mode_peer(d):
        return wrap(k + d, NK)

    fetches = [
        pltpu.make_async_copy(src, dst, fetch_sem.at[i])
        for i, (src, dst) in enumerate((
            (occ_hbm, occ_ref), (t0_hbm, t0_ref), (warm_hbm, warm_ref), (cour_hbm, cour_ref), (sign_hbm, sign_ref),
        ))
    ]
    for fetch in fetches:
        fetch.start()
    own = pltpu.make_async_copy(s_hbm, full.at[a, b], own_sem)
    own.start()
    barrier = pltpu.get_barrier_semaphore()

    @pl.loop(1, NK)
    def _(d):
        pl.semaphore_signal(barrier, inc=1, device_id=dev(s, mode_peer(d)), device_id_type=MESH)

    for peer in (right, left, z_peers[0], z_peers[2], z_pair, y_up, y_down):
        pl.semaphore_signal(barrier, inc=1, device_id=peer, device_id_type=MESH)

    pl.semaphore_wait(barrier, NK - 1 + 7)

    own.wait()
    rows = [a, wrap(a + toward, NA), wrap(a - toward, NA), wrap(a + 2, NA)]
    cols = [b, wrap(b - 1, NB), wrap(b + 1, NB), wrap(b + 2, NB)]
    parity = lax.rem(y + lo, 2)
    mine_u = parity * 4 + core * 2
    other_u = (1 - parity) * 4 + core * 2
    started = []

    def remote(block, send, recv, peer):
        return pltpu.make_async_remote_copy(
            src_ref=block, dst_ref=block, send_sem=send, recv_sem=recv, device_id=peer, device_id_type=MESH
        )

    def z_copy(n):
        block = full.at[a, b, pl.ds(mine_u if n == 2 else other_u, 2)]
        return remote(block, gz_send.at[n], gz_recv.at[n], z_peers[n - 1])

    def x_copy(n, step):
        if step < 2:
            block = full.at[rows[n], b, pl.ds(mine_u, 2)]
        else:
            block = full.at[rows[n], cols[step - 1], mine_u + step - 2]
        return remote(block, gx_send.at[n, step], gx_recv.at[n, step], x_down if step % 2 else x_up)

    def y_copy(n, m, way):
        block = full.at[rows[n], cols[m], mine_u + way]
        return remote(block, gy_send.at[n, m, way], gy_recv.at[n, m, way], y_down if way else y_up)

    def pair_copy(n, m):
        there = (0, 2, 1, 3)[n]
        return remote(full.at[rows[n], cols[m], pl.ds(mine_u, 2)], gp_send.at[n, m], gp_recv.at[there, m], z_pair)

    def core_copy(n, m, kind):
        block = full.at[rows[n], cols[m], pl.ds(other_u if kind else mine_u, 2)]
        return remote(block, c_send.at[n, m, kind], c_recv.at[n, m, kind], partner)

    def start(copy):
        copy.start()
        started.append(copy)

    def share(n, m):
        if m == 1:
            start(pair_copy(n, m))
        else:
            start(y_copy(n, m, 0))
            start(y_copy(n, m, 1))
        start(core_copy(n, m, 0))

    start(z_copy(1))
    start(x_copy(0, 0))
    start(x_copy(0, 1))
    start(z_copy(2))
    start(z_copy(3))

    def a2a(pairs, send, recv, d):
        return [
            pltpu.make_async_remote_copy(
                src_ref=src, dst_ref=dst, send_sem=send.at[d, i], recv_sem=recv.at[d, i],
                device_id=dev(s, mode_peer(d)), device_id_type=MESH,
            )
            for i, (src, dst) in enumerate(pairs)
        ]

    def a2a_in(d):
        block = block_of(mode_peer(d))
        pairs = (q_sent.at[block], q_state.at[k]), (coef_sent.at[block], coefs.at[k])
        return a2a(pairs, in_send, in_recv, d)

    def a2a_out(d):
        there = mode_peer(d)
        pairs = (q_final.at[there], q_landed.at[zb]), (tail.at[there], tails.at[zb])
        return a2a(pairs, o_send, o_recv, d)

    def quantized(values):
        most = jnp.max(jnp.abs(values), axis=0, keepdims=True)
        steps = jnp.where(most > 0.0, 32767.0 / most, 0.0)
        return jnp.round(values * steps).astype(jnp.int32).astype(jnp.int16), most * (1.0 / 32767.0)

    for fetch in fetches:
        fetch.wait()

    warm_col = jnp.transpose(jnp.broadcast_to(warm_ref[pl.ds(k, 1), :], (MODES, MODES)))
    for xy in range(8):
        cells = occ_ref[pl.ds(xy, MODES, stride=8), :] + warm_col * t0_ref[xy:xy + 1, :]
        sent[:, pl.ds(xy * 8, 8), :] = jnp.transpose(cells).reshape(NK, 8, MODES)
    sign = sign_ref[...]
    row = lax.broadcasted_iota(jnp.int32, (8, MODES), 0)
    coef = jnp.zeros((8, MODES), jnp.float32)
    for d in range(3):
        bit = jnp.broadcast_to((sign >> d) & 1, (8, MODES))
        c = jnp.broadcast_to(cour_ref[d:d + 1, :], (8, MODES))
        coef = jnp.where(row == 2 * d, jnp.where(bit == 0, c, 0.0), coef)
        coef = jnp.where(row == 2 * d + 1, jnp.where(bit == 1, c, 0.0), coef)

    @pl.loop(0, NK)
    def _(j):
        q, step = quantized(sent[j])
        q_sent[j] = q
        coef_sent[j] = jnp.where(row == 6, jnp.broadcast_to(step, (8, MODES)), coef)

    @pl.loop(1, NK)
    def _(d):
        for copy in a2a_in(d):
            copy.start()

    q_state[k] = q_sent[zb]
    coefs[k] = coef_sent[zb]

    def from_z(n):
        z_copy(n).wait_recv()
        start(x_copy(n, 0))
        start(x_copy(n, 1))
        share(n, 0)

    def from_x(n):
        for m in (1, 2):
            x_copy(n, m - 1).wait_recv()
            start(x_copy(n, m + 1))
        share(n, 1)
        share(n, 2)

    def from_far_x(n):
        x_copy(n, 2).wait_recv()
        x_copy(n, 3).wait_recv()
        share(n, 3)

    def from_others(n):
        for m in range(4):
            if n or m:
                if m == 1:
                    pair_copy((0, 2, 1, 3)[n], m).wait_recv()
                else:
                    y_copy(n, m, 0).wait_recv()
                    y_copy(n, m, 1).wait_recv()
                start(core_copy(n, m, 1))

    from_z(1)
    from_x(0)
    from_z(2)
    from_far_x(0)
    from_x(1)
    from_z(3)
    from_x(2)
    from_far_x(1)
    from_others(0)

    total = jnp.sum(warm_ref[...])
    zi = lax.broadcasted_iota(jnp.int32, (8, 8, MODES), 1)
    nt = (((1,), (1,)), ((), ()))
    H = NK // 2

    def halo_copies(t, h):
        part = pl.ds(h * H, H)
        return [
            pltpu.make_async_remote_copy(
                src_ref=src.at[t, way, part], dst_ref=dst.at[t, way, part],
                send_sem=send.at[t, way, h], recv_sem=recv.at[t, way, h], device_id=peer, device_id_type=MESH,
            )
            for src, dst, send, recv, peers in (
                (xs, xr, x_send, x_recv, (right, left)), (zs, zr, z_send, z_recv, (z_next, z_prev)),
            )
            for way, peer in enumerate(peers)
        ]

    def stage_halo(t, j):
        xs[t, 0, j] = state[j, 32:64, :].astype(jnp.bfloat16)
        xs[t, 1, j] = state[j, 0:32, :].astype(jnp.bfloat16)
        zs[t, 0, j] = state[j, pl.ds(7, 8, stride=8), :]
        zs[t, 1, j] = state[j, pl.ds(0, 8, stride=8), :]

    def send_halo(t, h):
        for copy in halo_copies(t, h):
            copy.start()

    def advect_block(t, j, energy):
        st = state[j].reshape(8, 8, MODES)
        cf = [coefs[j, pl.ds(r, 1), :].reshape(1, 1, MODES) for r in range(6)]
        below = xr[t, 0, j].astype(jnp.float32).reshape(4, 8, MODES)
        above = xr[t, 1, j].astype(jnp.float32).reshape(4, 8, MODES)
        x_below = jnp.concatenate([below, st[0:4]], axis=0)
        x_above = jnp.concatenate([st[4:8], above], axis=0)
        y_below = jnp.concatenate([st[3:4], st[0:3], st[7:8], st[4:7]], axis=0)
        y_above = jnp.concatenate([st[1:4], st[0:1], st[5:8], st[4:5]], axis=0)
        z_lower = zr[t, 0, j].reshape(8, 1, MODES)
        z_upper = zr[t, 1, j].reshape(8, 1, MODES)
        z_below = jnp.where(zi == 0, z_lower, jnp.roll(st, 1, 1))
        z_above = jnp.where(zi == 7, z_upper, jnp.roll(st, -1, 1))
        mv = st
        for d, (lower, upper) in enumerate(((x_below, x_above), (y_below, y_above), (z_below, z_above))):
            mv = mv - (cf[2 * d] * (st - lower) + cf[2 * d + 1] * (st - upper))
        mv = mv.reshape(64, MODES)
        mv_bf = mv.astype(jnp.bfloat16)
        moved[j] = mv
        lhs[:, pl.ds(pl.multiple_of(j * MODES, MODES), MODES)] = mv_bf
        return energy + mv_bf.astype(jnp.float32) * warm_ref[pl.ds(j, 1), :]

    def advect(t, h, energy):
        for copy in halo_copies(t, h):
            copy.wait_recv()
        return lax.fori_loop(h * H, h * H + H, functools.partial(advect_block, t), energy, unroll=4)

    def offset(energy):
        thermal = jnp.sum(energy, axis=1, keepdims=True) / total
        return jnp.broadcast_to(thermal, (64, MODES))

    nothing = jnp.zeros((64, MODES), jnp.float32)

    row16 = lax.broadcasted_iota(jnp.int32, (16, MODES), 0)
    for j in range(NK):
        w = jnp.broadcast_to(warm_ref[j:j + 1, :], (16, MODES))
        hi = w.astype(jnp.bfloat16).astype(jnp.float32)
        mid = (w - hi).astype(jnp.bfloat16).astype(jnp.float32)
        low = w - hi - mid
        parts = jnp.where(row16 == 0, hi, jnp.where(row16 == 1, mid, jnp.where(row16 == 2, low, 0.0)))
        wlhs[:, j * MODES:(j + 1) * MODES] = parts.astype(jnp.bfloat16)

    @pl.loop(1, NK)
    def _(d):
        for copy in a2a_in(d):
            copy.wait_recv()

    for h in range(2):
        @pl.loop(h * H, h * H + H)
        def _(j):
            state[j] = restored(q_state[j], coefs[j, 6:7])
            stage_halo(0, j)

        send_halo(0, h)

    from_x(3)
    from_far_x(2)
    from_others(1)
    thermal = offset(advect(0, 1, advect(0, 0, nothing)))

    def first_product(n):
        for m in range(4):
            if n or m:
                core_copy(n, m, 0).wait_recv()
                core_copy(n, m, 1).wait_recv()
        r = rows[n]
        w = full[r].reshape(4 * MODES, M)
        product = lax.dot_general(lhs[...], w, nt, preferred_element_type=jnp.float32)
        parts = lax.dot_general(wlhs[...], w, nt, preferred_element_type=jnp.float32)
        both = parts[0:1] + parts[1:2] + parts[2:3]
        for e in range(NB):
            j = r * NB + e
            rx = jnp.broadcast_to(both[:, e * MODES:(e + 1) * MODES], (8, MODES))
            relax[j] = rx
            state[j] = moved[j] - product[:, e * MODES:(e + 1) * MODES] + rx[0:1] * thermal
            stage_halo(1, j)

    from_far_x(3)
    first_product(0)
    from_others(2)
    first_product(1)
    first_product(2)
    from_others(3)
    first_product(3)


    for h in range(2):
        send_halo(1, h)

    for t in range(1, ITERS):
        last = t == ITERS - 1
        energy = advect(t, 0, nothing)

        @pl.loop(0, NA)
        def _(n):
            w = full[n, :, :, :, 0:M // 2].reshape(NB * MODES, M // 2)
            half[n] = lax.dot_general(lhs[:, 0:M // 2], w, nt, preferred_element_type=jnp.float32)

        thermal = offset(advect(t, 1, energy))
        if last:
            lane = lax.broadcasted_iota(jnp.int32, (64, MODES), 1)
            cell = lax.broadcasted_iota(jnp.int32, (64, MODES), 0)
            offsets = jnp.sum(jnp.where(lane == cell, thermal, 0.0), axis=0, keepdims=True)
            offsets = jnp.broadcast_to(offsets, (8, MODES))

        def finish(n):
            w = full[n, :, :, :, M // 2:M].reshape(NB * MODES, M // 2)
            product = half[n] + lax.dot_general(lhs[:, M // 2:M], w, nt, preferred_element_type=jnp.float32)
            for e in range(NB):
                j = NB * n + e
                new = moved[j] - product[:, e * MODES:(e + 1) * MODES] + relax[j, 0:1] * thermal
                if last:
                    q, step = quantized(new)
                    q_final[j] = q
                    tail[j] = jnp.where(row == 1, jnp.broadcast_to(step, (8, MODES)), offsets)
                    d = lax.rem(j - k + NK, NK)

                    @pl.when(d > 0)
                    def _():
                        for copy in a2a_out(d):
                            copy.start()
                else:
                    state[j] = new
                    stage_halo(t + 1, j)

        if last:
            @pl.loop(0, NA)
            def _(step):
                finish(wrap(a + step, NA))
        else:
            for h in range(2):
                @pl.loop(h * NA // 2, (h + 1) * NA // 2)
                def _(n):
                    finish(n)

                send_halo(t + 1, h)

    kept = [
        pltpu.make_async_copy(q_final.at[k], q_landed.at[zb], kept_sem.at[0]),
        pltpu.make_async_copy(tail.at[k], tails.at[zb], kept_sem.at[1]),
    ]
    for copy in kept:
        copy.start()
    for copy in kept:
        copy.wait()

    @pl.loop(1, NK)
    def _(d):
        for copy in a2a_out(d):
            copy.wait_recv()

    @pl.loop(1, NK)
    def _(d):
        for copy in a2a_in(d) + a2a_out(d):
            copy.wait_send()

    for copy in started:
        copy.wait_send()
    for t in range(ITERS):
        for h in range(2):
            for copy in halo_copies(t, h):
                copy.wait_send()


def restored(q, step):
    return q.astype(jnp.int32).astype(jnp.float32) * step


def unpack(q_ref, tail_ref, out_ref, therm_ref, back):
    @pl.loop(0, NK)
    def _(j):
        back[j] = restored(q_ref[j], tail_ref[j, 1:2]).reshape(8, 8, MODES)

    for xy in range(8):
        cells = back[:, xy].reshape(MODES, MODES)
        out_ref[pl.ds(xy, MODES, stride=8), :] = jnp.transpose(cells)
    lane = lax.broadcasted_iota(jnp.int32, (8, MODES), 1)
    offsets = jnp.zeros((8, MODES), jnp.float32)
    for j in range(NK):
        cells = jnp.broadcast_to(tail_ref[j, 0:1], (8, MODES))
        moved = pltpu.roll(cells, (8 * j - 56) % MODES, 1)
        moved = pltpu.roll(moved, 0, 1, stride=8, stride_axis=0)
        offsets = jnp.where(lane // 8 == j, moved, offsets)
    for xy in range(8):
        therm_ref[xy:xy + 1, :] = offsets[7 - xy:8 - xy]


def shards(occupation, offset, warmth, courant, sign, matrix):
    f32, bf16 = jnp.float32, jnp.bfloat16
    dma = pltpu.SemaphoreType.DMA
    vmem = pl.BlockSpec(memory_space=pltpu.VMEM)
    hbm = pl.BlockSpec(memory_space=pltpu.HBM)
    landed, tails = pl.pallas_call(
        kernel,
        out_shape=(
            jax.ShapeDtypeStruct((NK, 64, MODES), jnp.int16),
            jax.ShapeDtypeStruct((NK, 8, MODES), f32),
        ),
        in_specs=[hbm] * 6,
        out_specs=(hbm, hbm),
        scratch_shapes=[
            pltpu.VMEM((8 * MODES, 128), f32),
            pltpu.VMEM((8, 128), f32),
            pltpu.VMEM((NK, MODES), f32),
            pltpu.VMEM((3, MODES), f32),
            pltpu.VMEM((1, MODES), jnp.int32),
            pltpu.VMEM((NA, NB, 8, 16, M), bf16),
            pltpu.VMEM((NK, 64, MODES), f32),
            pltpu.VMEM((NK, 64, MODES), f32),
            pltpu.VMEM((NK, 64, MODES), jnp.int16),
            pltpu.VMEM((NK, 64, MODES), jnp.int16),
            pltpu.VMEM((NK, 8, MODES), f32),
            pltpu.VMEM((NK, 8, MODES), f32),
            pltpu.VMEM((NK, 64, MODES), jnp.int16),
            pltpu.VMEM((NK, 8, MODES), f32),
            pltpu.VMEM((64, M), bf16),
            pltpu.VMEM((16, M), bf16),
            pltpu.VMEM((NK, 8, MODES), f32),
            pltpu.VMEM((ITERS, 2, NK, 32, MODES), bf16),
            pltpu.VMEM((ITERS, 2, NK, 32, MODES), bf16),
            pltpu.VMEM((ITERS, 2, NK, 8, MODES), f32),
            pltpu.VMEM((ITERS, 2, NK, 8, MODES), f32),
            pltpu.VMEM((NK, 64, MODES), f32),
            pltpu.VMEM((NA, 64, NB * MODES), f32),
            dma((5,)),
            dma((2,)),
            dma,
            dma((4,)), dma((4,)),
            dma((4, 4)), dma((4, 4)),
            dma((4, 4, 2)), dma((4, 4, 2)),
            dma((4, 4)), dma((4, 4)),
            dma((4, 4, 2)), dma((4, 4, 2)),
            dma((NK, 2)), dma((NK, 2)),
            dma((ITERS, 2, 2)), dma((ITERS, 2, 2)),
            dma((ITERS, 2, 2)), dma((ITERS, 2, 2)),
            dma((NK, 2)), dma((NK, 2)),
        ],
        compiler_params=pltpu.CompilerParams(
            collective_id=0, has_side_effects=True, vmem_limit_bytes=62 * 1024 * 1024
        ),
        cost_estimate=pl.CostEstimate(flops=1_700_000_000, bytes_accessed=2_000_000, transcendentals=0),
    )(
        occupation.reshape(8 * MODES, 128),
        offset.reshape(8, 128),
        warmth.reshape(NK, MODES),
        courant,
        sign.reshape(1, MODES),
        matrix.reshape(8, 16, M),
    )
    out, therm = pl.pallas_call(
        unpack,
        out_shape=(
            jax.ShapeDtypeStruct((8 * MODES, 128), f32),
            jax.ShapeDtypeStruct((8, 128), f32),
        ),
        in_specs=[vmem, vmem],
        out_specs=(vmem, vmem),
        scratch_shapes=[pltpu.VMEM((NK, 8, 8, MODES), f32)],
    )(landed, tails)
    return out.reshape(occupation.shape), therm.reshape(offset.shape)


def solution(mesh):
    placed = (
        P("mode", "space", None, None),
        P("space", None, None),
        P(),
        P(None, "mode"),
        P("mode"),
        P("mode", None),
    )
    return jax.shard_map(
        shards,
        mesh=mesh,
        in_specs=placed,
        out_specs=(P("mode", "space", None, None), P("space", None, None)),
        check_vma=False,
    )
```

```python
import functools

import jax
import jax.numpy as jnp
from jax import lax
from jax.experimental import pallas as pl
from jax.experimental.pallas import tpu as pltpu
from jax.sharding import PartitionSpec as P

ITERS = 3
NA, NB = 4, 4
NK = NA * NB
NS = 32
MODES = 128
M = NK * MODES
MESH = pl.DeviceIdType.MESH

def kernel(
    occ_hbm, t0_hbm, warm_hbm, cour_hbm, sign_hbm, s_hbm,
    q_landed, tails,
    occ_ref, t0_ref, warm_ref, cour_ref, sign_ref,
    full, sent, state, q_sent, q_state, coef_sent, coefs, q_final, tail, lhs, wlhs, relax, xs, xr, zs, zr, moved, half,
    fetch_sem, kept_sem, own_sem, gz_send, gz_recv, gx_send, gx_recv, gf_send, gf_recv, gy_send, gy_recv, gp_send, gp_recv, c_send, c_recv, in_send, in_recv, x_send, x_recv, z_send, z_recv, o_send, o_recv,
):
    s = lax.axis_index("space")
    k = lax.axis_index("mode")
    a, b = k // NB, k % NB
    lo = s // 16
    core = s % 2

    def dev(space, mode):
        return {"space": space, "mode": mode}

    def wrap(v, n):
        return lax.rem(v + 4 * n, n)

    y = (s // 2) % 8
    toward = 2 * lo - 1
    z_near = dev(lax.rem(s + 16, NS), wrap(a + toward, NA) * NB + b)
    z_over = dev(s, wrap(a + toward, NA) * NB + b)
    z_back = dev(s, wrap(a - toward, NA) * NB + b)
    x_up, x_down = dev(s, a * NB + wrap(b + 1, NB)), dev(s, a * NB + wrap(b - 1, NB))
    z_pair = dev(lax.rem(s + 16, NS), k)
    y_up = dev(lo * 16 + wrap(y + 1, 8) * 2 + core, k)
    y_down = dev(lo * 16 + wrap(y - 1, 8) * 2 + core, k)
    partner = dev(s + 1 - 2 * core, k)
    right, left = dev(wrap(s + 1, NS), k), dev(wrap(s - 1, NS), k)

    def block_of(mode):
        aa, bb = mode // NB, mode % NB
        return aa * NB + bb + (aa % 2) * (NB - 1 - 2 * bb)

    zb = block_of(k)
    z_next, z_prev = dev(s, block_of(wrap(zb + 1, NK))), dev(s, block_of(wrap(zb - 1, NK)))

    def mode_peer(d):
        return wrap(k + d, NK)

    fetches = [
        pltpu.make_async_copy(src, dst, fetch_sem.at[i])
        for i, (src, dst) in enumerate((
            (occ_hbm, occ_ref), (t0_hbm, t0_ref), (warm_hbm, warm_ref), (cour_hbm, cour_ref), (sign_hbm, sign_ref),
        ))
    ]
    for fetch in fetches:
        fetch.start()
    own = pltpu.make_async_copy(s_hbm, full.at[a, b], own_sem)
    own.start()
    barrier = pltpu.get_barrier_semaphore()

    for peer in (right, left, z_near, z_pair, y_up, y_down):
        pl.semaphore_signal(barrier, inc=1, device_id=peer, device_id_type=MESH)

    @pl.loop(1, NK)
    def _(d):
        pl.semaphore_signal(barrier, inc=1, device_id=dev(s, mode_peer(d)), device_id_type=MESH)

    pl.semaphore_wait(barrier, NK - 1 + 6)

    own.wait()
    rows = [a, wrap(a + toward, NA), wrap(a - toward, NA), wrap(a + 2, NA)]
    cols = [b, wrap(b - 1, NB), wrap(b + 1, NB), wrap(b + 2, NB)]
    parity = lax.rem(y + lo, 2)
    mine_u = parity * 4 + core * 2
    other_u = (1 - parity) * 4 + core * 2
    started = []

    def remote(block, send, recv, peer):
        return pltpu.make_async_remote_copy(
            src_ref=block, dst_ref=block, send_sem=send, recv_sem=recv, device_id=peer, device_id_type=MESH
        )

    def z_copy(n):
        block = full.at[rows[1] if n == 3 else a, b, pl.ds(other_u if n == 1 else mine_u, 2)]
        return remote(block, gz_send.at[n], gz_recv.at[n], (z_near, z_over, z_back)[n - 1])

    def x_copy(n, way):
        block = full.at[rows[n], b, pl.ds(mine_u, 2)]
        return remote(block, gx_send.at[n, way], gx_recv.at[n, way], x_down if way else x_up)

    def far_copy(n, way):
        block = full.at[rows[n], cols[1 + way], mine_u + way]
        return remote(block, gf_send.at[n, way], gf_recv.at[n, way], x_down if way else x_up)

    def y_copy(n, m, way):
        block = full.at[rows[n], cols[m], mine_u + way]
        return remote(block, gy_send.at[n, m, way], gy_recv.at[n, m, way], y_down if way else y_up)

    def pair_copy(n, m):
        there = (0, 2, 1, 3)[n]
        return remote(full.at[rows[n], cols[m], pl.ds(mine_u, 2)], gp_send.at[n, m], gp_recv.at[there, m], z_pair)

    def core_copy(n, m, kind):
        block = full.at[rows[n], cols[m], pl.ds(other_u if kind else mine_u, 2)]
        return remote(block, c_send.at[n, m, kind], c_recv.at[n, m, kind], partner)

    def start(copy):
        copy.start()
        started.append(copy)

    def share(n, m):
        if m == 1:
            start(pair_copy(n, m))
        else:
            start(y_copy(n, m, 0))
            start(y_copy(n, m, 1))
        start(core_copy(n, m, 0))

    start(z_copy(1))
    start(x_copy(0, 0))
    start(x_copy(0, 1))
    start(z_copy(2))


    def a2a(pairs, send, recv, d):
        return [
            pltpu.make_async_remote_copy(
                src_ref=src, dst_ref=dst, send_sem=send.at[d, i], recv_sem=recv.at[d, i],
                device_id=dev(s, mode_peer(d)), device_id_type=MESH,
            )
            for i, (src, dst) in enumerate(pairs)
        ]

    def a2a_in(d):
        block = block_of(mode_peer(d))
        pairs = (q_sent.at[block], q_state.at[k]), (coef_sent.at[block], coefs.at[k])
        return a2a(pairs, in_send, in_recv, d)

    def a2a_out(d):
        there = mode_peer(d)
        pairs = (q_final.at[there], q_landed.at[zb]), (tail.at[there], tails.at[zb])
        return a2a(pairs, o_send, o_recv, d)

    def quantized(values):
        most = jnp.max(jnp.abs(values), axis=0, keepdims=True)
        steps = jnp.where(most > 0.0, 32767.0 / most, 0.0)
        return jnp.round(values * steps).astype(jnp.int32).astype(jnp.int16), most * (1.0 / 32767.0)

    for fetch in fetches:
        fetch.wait()

    warm_col = jnp.transpose(jnp.broadcast_to(warm_ref[pl.ds(k, 1), :], (MODES, MODES)))
    for xy in range(8):
        cells = occ_ref[pl.ds(xy, MODES, stride=8), :] + warm_col * t0_ref[xy:xy + 1, :]
        sent[:, pl.ds(xy * 8, 8), :] = jnp.transpose(cells).reshape(NK, 8, MODES)
    sign = sign_ref[...]
    row = lax.broadcasted_iota(jnp.int32, (8, MODES), 0)
    coef = jnp.zeros((8, MODES), jnp.float32)
    for d in range(3):
        bit = jnp.broadcast_to((sign >> d) & 1, (8, MODES))
        c = jnp.broadcast_to(cour_ref[d:d + 1, :], (8, MODES))
        coef = jnp.where(row == 2 * d, jnp.where(bit == 0, c, 0.0), coef)
        coef = jnp.where(row == 2 * d + 1, jnp.where(bit == 1, c, 0.0), coef)

    @pl.loop(0, NK)
    def _(j):
        q, step = quantized(sent[j])
        q_sent[j] = q
        coef_sent[j] = jnp.where(row == 6, jnp.broadcast_to(step, (8, MODES)), coef)

    @pl.loop(1, NK)
    def _(d):
        for copy in a2a_in(d):
            copy.start()

    q_state[k] = q_sent[zb]
    coefs[k] = coef_sent[zb]

    def from_z(n):
        z_copy(n).wait_recv()
        if n == 1:
            start(z_copy(3))
        start(x_copy(n, 0))
        start(x_copy(n, 1))
        share(n, 0)

    def from_x(n):
        for way in range(2):
            x_copy(n, way).wait_recv()
            start(far_copy(n, way))
        share(n, 1)
        share(n, 2)

    def from_far_x(n):
        far_copy(n, 0).wait_recv()
        far_copy(n, 1).wait_recv()
        share(n, 3)

    def from_others(n):
        for m in range(4):
            if n or m:
                if m == 1:
                    pair_copy((0, 2, 1, 3)[n], m).wait_recv()
                else:
                    y_copy(n, m, 0).wait_recv()
                    y_copy(n, m, 1).wait_recv()
                start(core_copy(n, m, 1))

    from_z(1)
    from_x(0)
    from_z(2)
    from_far_x(0)
    from_x(1)
    from_z(3)
    from_x(2)
    from_far_x(1)
    from_others(0)

    total = jnp.sum(warm_ref[...])
    zi = lax.broadcasted_iota(jnp.int32, (8, 8, MODES), 1)
    nt = (((1,), (1,)), ((), ()))

    def halo_copies(t, h):
        part = pl.ds(h * NB, NB)
        return [
            pltpu.make_async_remote_copy(
                src_ref=src.at[t, way, part], dst_ref=dst.at[t, way, part],
                send_sem=send.at[t, way, h], recv_sem=recv.at[t, way, h], device_id=peer, device_id_type=MESH,
            )
            for src, dst, send, recv, peers in (
                (xs, xr, x_send, x_recv, (right, left)), (zs, zr, z_send, z_recv, (z_next, z_prev)),
            )
            for way, peer in enumerate(peers)
        ]

    def stage_halo(t, j):
        xs[t, 0, j] = state[j, 32:64, :].astype(jnp.bfloat16)
        xs[t, 1, j] = state[j, 0:32, :].astype(jnp.bfloat16)
        zs[t, 0, j] = state[j, pl.ds(7, 8, stride=8), :]
        zs[t, 1, j] = state[j, pl.ds(0, 8, stride=8), :]

    def send_halo(t, h):
        for copy in halo_copies(t, h):
            copy.start()

    def advect_block(t, j, energy):
        st = state[j].reshape(8, 8, MODES)
        cf = [coefs[j, pl.ds(r, 1), :].reshape(1, 1, MODES) for r in range(6)]
        below = xr[t, 0, j].astype(jnp.float32).reshape(4, 8, MODES)
        above = xr[t, 1, j].astype(jnp.float32).reshape(4, 8, MODES)
        x_below = jnp.concatenate([below, st[0:4]], axis=0)
        x_above = jnp.concatenate([st[4:8], above], axis=0)
        y_below = jnp.concatenate([st[3:4], st[0:3], st[7:8], st[4:7]], axis=0)
        y_above = jnp.concatenate([st[1:4], st[0:1], st[5:8], st[4:5]], axis=0)
        z_lower = zr[t, 0, j].reshape(8, 1, MODES)
        z_upper = zr[t, 1, j].reshape(8, 1, MODES)
        z_below = jnp.where(zi == 0, z_lower, jnp.roll(st, 1, 1))
        z_above = jnp.where(zi == 7, z_upper, jnp.roll(st, -1, 1))
        mv = st
        for d, (lower, upper) in enumerate(((x_below, x_above), (y_below, y_above), (z_below, z_above))):
            mv = mv - (cf[2 * d] * (st - lower) + cf[2 * d + 1] * (st - upper))
        mv = mv.reshape(64, MODES)
        mv_bf = mv.astype(jnp.bfloat16)
        moved[j] = mv
        lhs[:, pl.ds(pl.multiple_of(j * MODES, MODES), MODES)] = mv_bf
        return energy + mv_bf.astype(jnp.float32) * warm_ref[pl.ds(j, 1), :]

    def advect(t, h, energy):
        for q in range(2 * h, 2 * h + 2):
            for copy in halo_copies(t, q):
                copy.wait_recv()
            energy = lax.fori_loop(q * NB, q * NB + NB, functools.partial(advect_block, t), energy, unroll=4)
        return energy

    def offset(energy):
        thermal = jnp.sum(energy, axis=1, keepdims=True) / total
        return jnp.broadcast_to(thermal, (64, MODES))

    nothing = jnp.zeros((64, MODES), jnp.float32)

    row16 = lax.broadcasted_iota(jnp.int32, (16, MODES), 0)
    for j in range(NK):
        w = jnp.broadcast_to(warm_ref[j:j + 1, :], (16, MODES))
        hi = w.astype(jnp.bfloat16).astype(jnp.float32)
        mid = (w - hi).astype(jnp.bfloat16).astype(jnp.float32)
        low = w - hi - mid
        parts = jnp.where(row16 == 0, hi, jnp.where(row16 == 1, mid, jnp.where(row16 == 2, low, 0.0)))
        wlhs[:, j * MODES:(j + 1) * MODES] = parts.astype(jnp.bfloat16)

    @pl.loop(1, NK)
    def _(d):
        for copy in a2a_in(d):
            copy.wait_recv()

    @pl.loop(0, NA)
    def _(q):
        @pl.loop(0, NB)
        def _(e):
            j = q * NB + e
            state[j] = restored(q_state[j], coefs[j, 6:7])
            stage_halo(0, j)

        send_halo(0, q)

    from_x(3)
    from_far_x(2)
    from_others(1)
    from_far_x(3)
    thermal = offset(advect(0, 1, advect(0, 0, nothing)))

    def first_product(n):
        for m in range(4):
            if n or m:
                core_copy(n, m, 0).wait_recv()
                core_copy(n, m, 1).wait_recv()
        r = rows[n]
        w = full[r].reshape(4 * MODES, M)
        product = lax.dot_general(lhs[...], w, nt, preferred_element_type=jnp.float32)
        parts = lax.dot_general(wlhs[...], w, nt, preferred_element_type=jnp.float32)
        both = parts[0:1] + parts[1:2] + parts[2:3]
        for e in range(NB):
            j = r * NB + e
            rx = jnp.broadcast_to(both[:, e * MODES:(e + 1) * MODES], (8, MODES))
            relax[j] = rx
            state[j] = moved[j] - product[:, e * MODES:(e + 1) * MODES] + rx[0:1] * thermal
            stage_halo(1, j)
        send_halo(1, r)

    first_product(0)
    from_others(2)
    first_product(1)
    first_product(2)
    from_others(3)
    first_product(3)


    for t in range(1, ITERS):
        last = t == ITERS - 1
        energy = advect(t, 0, nothing)
        order = [cols[3], cols[2], cols[1], b] if last else list(range(NB))

        def weights(n, h):
            part = slice(h * (M // 2), (h + 1) * (M // 2))
            return jnp.concatenate([full[n, c, :, :, part].reshape(MODES, M // 2) for c in order], axis=0)

        @pl.loop(0, NA)
        def _(n):
            w = weights(n, 0)
            half[n] = lax.dot_general(lhs[:, 0:M // 2], w, nt, preferred_element_type=jnp.float32)

        thermal = offset(advect(t, 1, energy))
        if last:
            lane = lax.broadcasted_iota(jnp.int32, (64, MODES), 1)
            cell = lax.broadcasted_iota(jnp.int32, (64, MODES), 0)
            offsets = jnp.sum(jnp.where(lane == cell, thermal, 0.0), axis=0, keepdims=True)

        def finish(n):
            w = weights(n, 1)
            product = half[n] + lax.dot_general(lhs[:, M // 2:M], w, nt, preferred_element_type=jnp.float32)
            for e in range(NB):
                j = NB * n + order[e]
                new = moved[j] - product[:, e * MODES:(e + 1) * MODES] + relax[j, 0:1] * thermal
                if last:
                    q, step = quantized(new)
                    q_final[j] = q
                    tail[j] = jnp.concatenate([offsets, step], axis=0)
                    d = lax.rem(j - k + NK, NK)

                    @pl.when(d > 0)
                    def _():
                        for copy in a2a_out(d):
                            copy.start()
                else:
                    state[j] = new
                    stage_halo(t + 1, j)

        if last:
            @pl.loop(0, NA)
            def _(step):
                finish(wrap(a + 2 + step - 3 * (step // 2) - 2 * (step // 3), NA))
        else:
            @pl.loop(0, NA)
            def _(n):
                finish(n)
                send_halo(t + 1, n)

    kept = [
        pltpu.make_async_copy(q_final.at[k], q_landed.at[zb], kept_sem.at[0]),
        pltpu.make_async_copy(tail.at[k], tails.at[zb], kept_sem.at[1]),
    ]
    for copy in kept:
        copy.start()
    for copy in kept:
        copy.wait()

    @pl.loop(1, NK)
    def _(d):
        for copy in a2a_out(d):
            copy.wait_recv()

    @pl.loop(1, NK)
    def _(d):
        for copy in a2a_in(d) + a2a_out(d):
            copy.wait_send()

    for copy in started:
        copy.wait_send()
    for t in range(ITERS):
        for h in range(NA):
            for copy in halo_copies(t, h):
                copy.wait_send()


def restored(q, step):
    return q.astype(jnp.int32).astype(jnp.float32) * step


def unpack(q_ref, tail_ref, out_ref, therm_ref, back):
    @pl.loop(0, NK)
    def _(j):
        back[j] = restored(q_ref[j], tail_ref[j, 1:2]).reshape(8, 8, MODES)

    for xy in range(8):
        cells = back[:, xy].reshape(MODES, MODES)
        out_ref[pl.ds(xy, MODES, stride=8), :] = jnp.transpose(cells)
    lane = lax.broadcasted_iota(jnp.int32, (8, MODES), 1)
    offsets = jnp.zeros((8, MODES), jnp.float32)
    for j in range(NK):
        cells = jnp.broadcast_to(tail_ref[j, 0:1], (8, MODES))
        moved = pltpu.roll(cells, (8 * j - 56) % MODES, 1)
        moved = pltpu.roll(moved, 0, 1, stride=8, stride_axis=0)
        offsets = jnp.where(lane // 8 == j, moved, offsets)
    for xy in range(8):
        therm_ref[xy:xy + 1, :] = offsets[7 - xy:8 - xy]


def shards(occupation, offset, warmth, courant, sign, matrix):
    f32, bf16 = jnp.float32, jnp.bfloat16
    dma = pltpu.SemaphoreType.DMA
    vmem = pl.BlockSpec(memory_space=pltpu.VMEM)
    hbm = pl.BlockSpec(memory_space=pltpu.HBM)
    landed, tails = pl.pallas_call(
        kernel,
        out_shape=(
            jax.ShapeDtypeStruct((NK, 64, MODES), jnp.int16),
            jax.ShapeDtypeStruct((NK, 2, MODES), f32),
        ),
        in_specs=[hbm] * 6,
        out_specs=(hbm, hbm),
        scratch_shapes=[
            pltpu.VMEM((8 * MODES, 128), f32),
            pltpu.VMEM((8, 128), f32),
            pltpu.VMEM((NK, MODES), f32),
            pltpu.VMEM((3, MODES), f32),
            pltpu.VMEM((1, MODES), jnp.int32),
            pltpu.VMEM((NA, NB, 8, 16, M), bf16),
            pltpu.VMEM((NK, 64, MODES), f32),
            pltpu.VMEM((NK, 64, MODES), f32),
            pltpu.VMEM((NK, 64, MODES), jnp.int16),
            pltpu.VMEM((NK, 64, MODES), jnp.int16),
            pltpu.VMEM((NK, 8, MODES), f32),
            pltpu.VMEM((NK, 8, MODES), f32),
            pltpu.VMEM((NK, 64, MODES), jnp.int16),
            pltpu.VMEM((NK, 2, MODES), f32),
            pltpu.VMEM((64, M), bf16),
            pltpu.VMEM((16, M), bf16),
            pltpu.VMEM((NK, 8, MODES), f32),
            pltpu.VMEM((ITERS, 2, NK, 32, MODES), bf16),
            pltpu.VMEM((ITERS, 2, NK, 32, MODES), bf16),
            pltpu.VMEM((ITERS, 2, NK, 8, MODES), f32),
            pltpu.VMEM((ITERS, 2, NK, 8, MODES), f32),
            pltpu.VMEM((NK, 64, MODES), f32),
            pltpu.VMEM((NA, 64, NB * MODES), f32),
            dma((5,)),
            dma((2,)),
            dma,
            dma((4,)), dma((4,)),
            dma((4, 2)), dma((4, 2)),
            dma((4, 2)), dma((4, 2)),
            dma((4, 4, 2)), dma((4, 4, 2)),
            dma((4, 4)), dma((4, 4)),
            dma((4, 4, 2)), dma((4, 4, 2)),
            dma((NK, 2)), dma((NK, 2)),
            dma((ITERS, 2, NA)), dma((ITERS, 2, NA)),
            dma((ITERS, 2, NA)), dma((ITERS, 2, NA)),
            dma((NK, 2)), dma((NK, 2)),
        ],
        compiler_params=pltpu.CompilerParams(
            collective_id=0, has_side_effects=True, vmem_limit_bytes=62 * 1024 * 1024
        ),
        cost_estimate=pl.CostEstimate(flops=1_700_000_000, bytes_accessed=2_000_000, transcendentals=0),
    )(
        occupation.reshape(8 * MODES, 128),
        offset.reshape(8, 128),
        warmth.reshape(NK, MODES),
        courant,
        sign.reshape(1, MODES),
        matrix.reshape(8, 16, M),
    )
    out, therm = pl.pallas_call(
        unpack,
        out_shape=(
            jax.ShapeDtypeStruct((8 * MODES, 128), f32),
            jax.ShapeDtypeStruct((8, 128), f32),
        ),
        in_specs=[vmem, vmem],
        out_specs=(vmem, vmem),
        scratch_shapes=[pltpu.VMEM((NK, 8, 8, MODES), f32)],
    )(landed, tails)
    return out.reshape(occupation.shape), therm.reshape(offset.shape)


def solution(mesh):
    placed = (
        P("mode", "space", None, None),
        P("space", None, None),
        P(),
        P(None, "mode"),
        P("mode"),
        P("mode", None),
    )
    return jax.shard_map(
        shards,
        mesh=mesh,
        in_specs=placed,
        out_specs=(P("mode", "space", None, None), P("space", None, None)),
        check_vma=False,
    )
```

```python
import functools

import jax
import jax.numpy as jnp
from jax import lax
from jax.experimental import pallas as pl
from jax.experimental.pallas import tpu as pltpu
from jax.sharding import PartitionSpec as P

ITERS = 3
NA, NB = 4, 4
NK = NA * NB
NS = 32
MODES = 128
M = NK * MODES
MESH = pl.DeviceIdType.MESH

def kernel(
    occ_hbm, t0_hbm, warm_hbm, cour_hbm, sign_hbm, s_hbm,
    q_landed, tails,
    occ_ref, t0_ref, warm_ref, cour_ref, sign_ref,
    full, sent, state, q_sent, q_state, coef_sent, coefs, q_final, tail, lhs, wlhs, relax, xs, xr, zs, zr, moved, half,
    fetch_sem, kept_sem, own_sem, gz_send, gz_recv, gx_send, gx_recv, gf_send, gf_recv, gy_send, gy_recv, gp_send, gp_recv, c_send, c_recv, in_send, in_recv, x_send, x_recv, z_send, z_recv, o_send, o_recv,
):
    s = lax.axis_index("space")
    k = lax.axis_index("mode")
    a, b = k // NB, k % NB
    lo = s // 16
    core = s % 2

    def dev(space, mode):
        return {"space": space, "mode": mode}

    def wrap(v, n):
        return lax.rem(v + 4 * n, n)

    y = (s // 2) % 8
    toward = 2 * lo - 1
    z_near = dev(lax.rem(s + 16, NS), wrap(a + toward, NA) * NB + b)
    z_over = dev(s, wrap(a + toward, NA) * NB + b)
    z_back = dev(s, wrap(a - toward, NA) * NB + b)
    x_up, x_down = dev(s, a * NB + wrap(b + 1, NB)), dev(s, a * NB + wrap(b - 1, NB))
    z_pair = dev(lax.rem(s + 16, NS), k)
    y_up = dev(lo * 16 + wrap(y + 1, 8) * 2 + core, k)
    y_down = dev(lo * 16 + wrap(y - 1, 8) * 2 + core, k)
    partner = dev(s + 1 - 2 * core, k)
    right, left = dev(wrap(s + 1, NS), k), dev(wrap(s - 1, NS), k)

    def block_of(mode):
        aa, bb = mode // NB, mode % NB
        return aa * NB + bb + (aa % 2) * (NB - 1 - 2 * bb)

    zb = block_of(k)
    z_next, z_prev = dev(s, block_of(wrap(zb + 1, NK))), dev(s, block_of(wrap(zb - 1, NK)))

    def mode_peer(d):
        return wrap(k + d, NK)

    fetches = [
        pltpu.make_async_copy(src, dst, fetch_sem.at[i])
        for i, (src, dst) in enumerate((
            (occ_hbm, occ_ref), (t0_hbm, t0_ref), (warm_hbm, warm_ref), (cour_hbm, cour_ref), (sign_hbm, sign_ref),
        ))
    ]
    for fetch in fetches:
        fetch.start()
    own = pltpu.make_async_copy(s_hbm, full.at[a, b], own_sem)
    own.start()
    barrier = pltpu.get_barrier_semaphore()

    for peer in (right, left, z_near, z_pair, y_up, y_down):
        pl.semaphore_signal(barrier, inc=1, device_id=peer, device_id_type=MESH)

    @pl.loop(1, NK, unroll=3)
    def _(d):
        pl.semaphore_signal(barrier, inc=1, device_id=dev(s, mode_peer(d)), device_id_type=MESH)

    pl.semaphore_wait(barrier, NK - 1 + 6)

    own.wait()
    rows = [a, wrap(a + toward, NA), wrap(a - toward, NA), wrap(a + 2, NA)]
    cols = [b, wrap(b - 1, NB), wrap(b + 1, NB), wrap(b + 2, NB)]
    parity = lax.rem(y + lo, 2)
    mine_u = parity * 4 + core * 2
    other_u = (1 - parity) * 4 + core * 2
    started = []

    def remote(block, send, recv, peer):
        return pltpu.make_async_remote_copy(
            src_ref=block, dst_ref=block, send_sem=send, recv_sem=recv, device_id=peer, device_id_type=MESH
        )

    def z_copy(n):
        block = full.at[rows[1] if n == 3 else a, b, pl.ds(other_u if n == 1 else mine_u, 2)]
        return remote(block, gz_send.at[n], gz_recv.at[n], (z_near, z_over, z_back)[n - 1])

    def x_copy(n, way):
        block = full.at[rows[n], b, pl.ds(mine_u, 2)]
        return remote(block, gx_send.at[n, way], gx_recv.at[n, way], x_down if way else x_up)

    def far_copy(n, way):
        block = full.at[rows[n], cols[1 + way], mine_u + way]
        return remote(block, gf_send.at[n, way], gf_recv.at[n, way], x_down if way else x_up)

    def y_copy(n, m, way):
        block = full.at[rows[n], cols[m], mine_u + way]
        return remote(block, gy_send.at[n, m, way], gy_recv.at[n, m, way], y_down if way else y_up)

    def pair_copy(n, m):
        there = (0, 2, 1, 3)[n]
        return remote(full.at[rows[n], cols[m], pl.ds(mine_u, 2)], gp_send.at[n, m], gp_recv.at[there, m], z_pair)

    def core_copy(n, m, kind):
        block = full.at[rows[n], cols[m], pl.ds(other_u if kind else mine_u, 2)]
        return remote(block, c_send.at[n, m, kind], c_recv.at[n, m, kind], partner)

    def start(copy):
        copy.start()
        started.append(copy)

    def share(n, m):
        if m == 1:
            start(pair_copy(n, m))
        else:
            start(y_copy(n, m, 0))
            start(y_copy(n, m, 1))
        start(core_copy(n, m, 0))

    start(z_copy(1))
    start(x_copy(0, 0))
    start(x_copy(0, 1))
    start(z_copy(2))


    def a2a(pairs, send, recv, d):
        return [
            pltpu.make_async_remote_copy(
                src_ref=src, dst_ref=dst, send_sem=send.at[d, i], recv_sem=recv.at[d, i],
                device_id=dev(s, mode_peer(d)), device_id_type=MESH,
            )
            for i, (src, dst) in enumerate(pairs)
        ]

    def a2a_in(d):
        block = block_of(mode_peer(d))
        pairs = (q_sent.at[block], q_state.at[k]), (coef_sent.at[block], coefs.at[k])
        return a2a(pairs, in_send, in_recv, d)

    def a2a_out(d):
        there = mode_peer(d)
        pairs = (q_final.at[there], q_landed.at[zb]), (tail.at[there], tails.at[zb])
        return a2a(pairs, o_send, o_recv, d)

    def quantized(values):
        most = jnp.max(jnp.abs(values), axis=0, keepdims=True)
        steps = jnp.where(most > 0.0, 32767.0 / most, 0.0)
        return jnp.round(values * steps).astype(jnp.int32).astype(jnp.int16), most * (1.0 / 32767.0)

    for fetch in fetches:
        fetch.wait()

    warm_col = jnp.transpose(jnp.broadcast_to(warm_ref[pl.ds(k, 1), :], (MODES, MODES)))
    for xy in range(8):
        cells = occ_ref[pl.ds(xy, MODES, stride=8), :] + warm_col * t0_ref[xy:xy + 1, :]
        sent[:, pl.ds(xy * 8, 8), :] = jnp.transpose(cells).reshape(NK, 8, MODES)
    sign = sign_ref[...]
    row = lax.broadcasted_iota(jnp.int32, (8, MODES), 0)
    coef = jnp.zeros((8, MODES), jnp.float32)
    for d in range(3):
        bit = jnp.broadcast_to((sign >> d) & 1, (8, MODES))
        c = jnp.broadcast_to(cour_ref[d:d + 1, :], (8, MODES))
        coef = jnp.where(row == 2 * d, jnp.where(bit == 0, c, 0.0), coef)
        coef = jnp.where(row == 2 * d + 1, jnp.where(bit == 1, c, 0.0), coef)

    @pl.loop(0, NK)
    def _(j):
        q, step = quantized(sent[j])
        q_sent[j] = q
        coef_sent[j] = jnp.where(row == 6, jnp.broadcast_to(step, (8, MODES)), coef)

    q_state[k] = q_sent[zb]
    coefs[k] = coef_sent[zb]

    def from_z(n):
        z_copy(n).wait_recv()
        if n == 1:
            start(z_copy(3))
        start(x_copy(n, 0))
        start(x_copy(n, 1))
        share(n, 0)

    def from_x(n):
        for way in range(2):
            x_copy(n, way).wait_recv()
            start(far_copy(n, way))
        share(n, 1)
        share(n, 2)

    def from_far_x(n):
        far_copy(n, 0).wait_recv()
        far_copy(n, 1).wait_recv()
        share(n, 3)

    def from_others(n):
        for m in range(4):
            if n or m:
                if m == 1:
                    pair_copy((0, 2, 1, 3)[n], m).wait_recv()
                else:
                    y_copy(n, m, 0).wait_recv()
                    y_copy(n, m, 1).wait_recv()
                start(core_copy(n, m, 1))

    from_z(1)
    from_x(0)

    @pl.loop(1, NK, unroll=3)
    def _(d):
        for copy in a2a_in(lax.rem(d + 6, NK - 1) + 1):
            copy.start()

    from_z(2)
    from_far_x(0)
    from_x(1)
    from_z(3)
    from_x(2)
    from_far_x(1)
    from_others(0)

    total = jnp.sum(warm_ref[...])
    zi = lax.broadcasted_iota(jnp.int32, (8, 8, MODES), 1)
    nt = (((1,), (1,)), ((), ()))

    def halo_copies(t, h):
        part = pl.ds(h * NB, NB)
        return [
            pltpu.make_async_remote_copy(
                src_ref=src.at[t, way, part], dst_ref=dst.at[t, way, part],
                send_sem=send.at[t, way, h], recv_sem=recv.at[t, way, h], device_id=peer, device_id_type=MESH,
            )
            for src, dst, send, recv, peers in (
                (xs, xr, x_send, x_recv, (right, left)), (zs, zr, z_send, z_recv, (z_next, z_prev)),
            )
            for way, peer in enumerate(peers)
        ]

    def stage_halo(t, j):
        xs[t, 0, j] = state[j, 32:64, :].astype(jnp.bfloat16)
        xs[t, 1, j] = state[j, 0:32, :].astype(jnp.bfloat16)
        zs[t, 0, j] = state[j, pl.ds(7, 8, stride=8), :]
        zs[t, 1, j] = state[j, pl.ds(0, 8, stride=8), :]

    def send_halo(t, h):
        for copy in halo_copies(t, h):
            copy.start()

    def advect_block(t, j, energy):
        st = state[j].reshape(8, 8, MODES)
        cf = [coefs[j, pl.ds(r, 1), :].reshape(1, 1, MODES) for r in range(6)]
        below = xr[t, 0, j].astype(jnp.float32).reshape(4, 8, MODES)
        above = xr[t, 1, j].astype(jnp.float32).reshape(4, 8, MODES)
        x_below = jnp.concatenate([below, st[0:4]], axis=0)
        x_above = jnp.concatenate([st[4:8], above], axis=0)
        y_below = jnp.concatenate([st[3:4], st[0:3], st[7:8], st[4:7]], axis=0)
        y_above = jnp.concatenate([st[1:4], st[0:1], st[5:8], st[4:5]], axis=0)
        z_lower = zr[t, 0, j].reshape(8, 1, MODES)
        z_upper = zr[t, 1, j].reshape(8, 1, MODES)
        z_below = jnp.where(zi == 0, z_lower, jnp.roll(st, 1, 1))
        z_above = jnp.where(zi == 7, z_upper, jnp.roll(st, -1, 1))
        mv = st
        for d, (lower, upper) in enumerate(((x_below, x_above), (y_below, y_above), (z_below, z_above))):
            mv = mv - (cf[2 * d] * (st - lower) + cf[2 * d + 1] * (st - upper))
        mv = mv.reshape(64, MODES)
        mv_bf = mv.astype(jnp.bfloat16)
        moved[j] = mv
        lhs[:, pl.ds(pl.multiple_of(j * MODES, MODES), MODES)] = mv_bf
        return energy + mv_bf.astype(jnp.float32) * warm_ref[pl.ds(j, 1), :]

    def advect(t, h, energy):
        for q in range(2 * h, 2 * h + 2):
            for copy in halo_copies(t, q):
                copy.wait_recv()
            energy = lax.fori_loop(q * NB, q * NB + NB, functools.partial(advect_block, t), energy, unroll=4)
        return energy

    def offset(energy):
        thermal = jnp.sum(energy, axis=1, keepdims=True) / total
        return jnp.broadcast_to(thermal, (64, MODES))

    nothing = jnp.zeros((64, MODES), jnp.float32)

    row16 = lax.broadcasted_iota(jnp.int32, (16, MODES), 0)
    for j in range(NK):
        w = jnp.broadcast_to(warm_ref[j:j + 1, :], (16, MODES))
        hi = w.astype(jnp.bfloat16).astype(jnp.float32)
        mid = (w - hi).astype(jnp.bfloat16).astype(jnp.float32)
        low = w - hi - mid
        parts = jnp.where(row16 == 0, hi, jnp.where(row16 == 1, mid, jnp.where(row16 == 2, low, 0.0)))
        wlhs[:, j * MODES:(j + 1) * MODES] = parts.astype(jnp.bfloat16)

    @pl.loop(1, NK, unroll=3)
    def _(d):
        for copy in a2a_in(d):
            copy.wait_recv()

    @pl.loop(0, NA)
    def _(q):
        @pl.loop(0, NB)
        def _(e):
            j = q * NB + e
            state[j] = restored(q_state[j], coefs[j, 6:7])
            stage_halo(0, j)

        send_halo(0, q)

    from_x(3)
    from_far_x(2)
    from_others(1)
    from_far_x(3)
    thermal = offset(advect(0, 1, advect(0, 0, nothing)))

    def first_product(n):
        for m in range(4):
            if n or m:
                core_copy(n, m, 0).wait_recv()
                core_copy(n, m, 1).wait_recv()
        r = rows[n]
        w = full[r].reshape(4 * MODES, M)
        product = lax.dot_general(lhs[...], w, nt, preferred_element_type=jnp.float32)
        parts = lax.dot_general(wlhs[...], w, nt, preferred_element_type=jnp.float32)
        both = parts[0:1] + parts[1:2] + parts[2:3]
        for e in range(NB):
            j = r * NB + e
            rx = jnp.broadcast_to(both[:, e * MODES:(e + 1) * MODES], (8, MODES))
            relax[j] = rx
            state[j] = moved[j] - product[:, e * MODES:(e + 1) * MODES] + rx[0:1] * thermal
            stage_halo(1, j)
        send_halo(1, r)

    first_product(0)
    from_others(2)
    first_product(1)
    first_product(2)
    from_others(3)
    first_product(3)


    def halos_left(t):
        for q in range(NA):
            for copy in halo_copies(t, q):
                copy.wait_send()

    for copy in started:
        copy.wait_send()

    @pl.loop(1, NK, unroll=3)
    def _(d):
        for copy in a2a_in(d):
            copy.wait_send()

    halos_left(0)

    for t in range(1, ITERS):
        last = t == ITERS - 1
        if t > 1:
            halos_left(t - 1)
        energy = advect(t, 0, nothing)
        order = [cols[3], cols[2], cols[1], b] if last else list(range(NB))

        def weights(n, h):
            part = slice(h * (M // 2), (h + 1) * (M // 2))
            return jnp.concatenate([full[n, c, :, :, part].reshape(MODES, M // 2) for c in order], axis=0)

        @pl.loop(0, NA, unroll=2)
        def _(n):
            w = weights(n, 0)
            half[n] = lax.dot_general(lhs[:, 0:M // 2], w, nt, preferred_element_type=jnp.float32)

        thermal = offset(advect(t, 1, energy))
        if last:
            lane = lax.broadcasted_iota(jnp.int32, (64, MODES), 1)
            cell = lax.broadcasted_iota(jnp.int32, (64, MODES), 0)
            offsets = jnp.sum(jnp.where(lane == cell, thermal, 0.0), axis=0, keepdims=True)

        def finish(n, own_row=False):
            w = weights(n, 1)
            product = half[n] + lax.dot_general(lhs[:, M // 2:M], w, nt, preferred_element_type=jnp.float32)
            for e in range(NB):
                j = NB * n + order[e]
                new = moved[j] - product[:, e * MODES:(e + 1) * MODES] + relax[j, 0:1] * thermal
                if last:
                    q, step = quantized(new)
                    q_final[j] = q
                    tail[j] = jnp.concatenate([offsets, step], axis=0)
                    if not (own_row and e == NB - 1):
                        for copy in a2a_out(lax.rem(j - k + NK, NK)):
                            copy.start()
                else:
                    state[j] = new
                    stage_halo(t + 1, j)

        if last:
            for step in (2, 1, 3, 0):
                finish(wrap(a + step, NA), step == 0)
        else:
            @pl.loop(0, NA, unroll=2)
            def _(n):
                finish(n)
                send_halo(t + 1, n)

    kept = [
        pltpu.make_async_copy(q_final.at[k], q_landed.at[zb], kept_sem.at[0]),
        pltpu.make_async_copy(tail.at[k], tails.at[zb], kept_sem.at[1]),
    ]
    for copy in kept:
        copy.start()
    halos_left(ITERS - 1)
    for copy in kept:
        copy.wait()

    @pl.loop(1, NK, unroll=3)
    def _(d):
        for copy in a2a_out(d):
            copy.wait_recv()

    @pl.loop(1, NK, unroll=3)
    def _(d):
        for copy in a2a_out(d):
            copy.wait_send()


def restored(q, step):
    return q.astype(jnp.int32).astype(jnp.float32) * step


def unpack(q_ref, tail_ref, out_ref, therm_ref, back):
    @pl.loop(0, NK)
    def _(j):
        back[j] = restored(q_ref[j], tail_ref[j, 1:2]).reshape(8, 8, MODES)

    for xy in range(8):
        cells = back[:, xy].reshape(MODES, MODES)
        out_ref[pl.ds(xy, MODES, stride=8), :] = jnp.transpose(cells)
    lane = lax.broadcasted_iota(jnp.int32, (8, MODES), 1)
    offsets = jnp.zeros((8, MODES), jnp.float32)
    for j in range(NK):
        cells = jnp.broadcast_to(tail_ref[j, 0:1], (8, MODES))
        moved = pltpu.roll(cells, (8 * j - 56) % MODES, 1)
        moved = pltpu.roll(moved, 0, 1, stride=8, stride_axis=0)
        offsets = jnp.where(lane // 8 == j, moved, offsets)
    for xy in range(8):
        therm_ref[xy:xy + 1, :] = offsets[7 - xy:8 - xy]


def shards(occupation, offset, warmth, courant, sign, matrix):
    f32, bf16 = jnp.float32, jnp.bfloat16
    dma = pltpu.SemaphoreType.DMA
    vmem = pl.BlockSpec(memory_space=pltpu.VMEM)
    hbm = pl.BlockSpec(memory_space=pltpu.HBM)
    landed, tails = pl.pallas_call(
        kernel,
        out_shape=(
            jax.ShapeDtypeStruct((NK, 64, MODES), jnp.int16),
            jax.ShapeDtypeStruct((NK, 2, MODES), f32),
        ),
        in_specs=[hbm] * 6,
        out_specs=(hbm, hbm),
        scratch_shapes=[
            pltpu.VMEM((8 * MODES, 128), f32),
            pltpu.VMEM((8, 128), f32),
            pltpu.VMEM((NK, MODES), f32),
            pltpu.VMEM((3, MODES), f32),
            pltpu.VMEM((1, MODES), jnp.int32),
            pltpu.VMEM((NA, NB, 8, 16, M), bf16),
            pltpu.VMEM((NK, 64, MODES), f32),
            pltpu.VMEM((NK, 64, MODES), f32),
            pltpu.VMEM((NK, 64, MODES), jnp.int16),
            pltpu.VMEM((NK, 64, MODES), jnp.int16),
            pltpu.VMEM((NK, 8, MODES), f32),
            pltpu.VMEM((NK, 8, MODES), f32),
            pltpu.VMEM((NK, 64, MODES), jnp.int16),
            pltpu.VMEM((NK, 2, MODES), f32),
            pltpu.VMEM((64, M), bf16),
            pltpu.VMEM((16, M), bf16),
            pltpu.VMEM((NK, 8, MODES), f32),
            pltpu.VMEM((ITERS, 2, NK, 32, MODES), bf16),
            pltpu.VMEM((ITERS, 2, NK, 32, MODES), bf16),
            pltpu.VMEM((ITERS, 2, NK, 8, MODES), f32),
            pltpu.VMEM((ITERS, 2, NK, 8, MODES), f32),
            pltpu.VMEM((NK, 64, MODES), f32),
            pltpu.VMEM((NA, 64, NB * MODES), f32),
            dma((5,)),
            dma((2,)),
            dma,
            dma((4,)), dma((4,)),
            dma((4, 2)), dma((4, 2)),
            dma((4, 2)), dma((4, 2)),
            dma((4, 4, 2)), dma((4, 4, 2)),
            dma((4, 4)), dma((4, 4)),
            dma((4, 4, 2)), dma((4, 4, 2)),
            dma((NK, 2)), dma((NK, 2)),
            dma((ITERS, 2, NA)), dma((ITERS, 2, NA)),
            dma((ITERS, 2, NA)), dma((ITERS, 2, NA)),
            dma((NK, 2)), dma((NK, 2)),
        ],
        compiler_params=pltpu.CompilerParams(
            collective_id=0, has_side_effects=True, vmem_limit_bytes=62 * 1024 * 1024
        ),
        cost_estimate=pl.CostEstimate(flops=1_700_000_000, bytes_accessed=2_000_000, transcendentals=0),
    )(
        occupation.reshape(8 * MODES, 128),
        offset.reshape(8, 128),
        warmth.reshape(NK, MODES),
        courant,
        sign.reshape(1, MODES),
        matrix.reshape(8, 16, M),
    )
    out, therm = pl.pallas_call(
        unpack,
        out_shape=(
            jax.ShapeDtypeStruct((8 * MODES, 128), f32),
            jax.ShapeDtypeStruct((8, 128), f32),
        ),
        in_specs=[vmem, vmem],
        out_specs=(vmem, vmem),
        scratch_shapes=[pltpu.VMEM((NK, 8, 8, MODES), f32)],
    )(landed, tails)
    return out.reshape(occupation.shape), therm.reshape(offset.shape)


def solution(mesh):
    placed = (
        P("mode", "space", None, None),
        P("space", None, None),
        P(),
        P(None, "mode"),
        P("mode"),
        P("mode", None),
    )
    return jax.shard_map(
        shards,
        mesh=mesh,
        in_specs=placed,
        out_specs=(P("mode", "space", None, None), P("space", None, None)),
        check_vma=False,
    )
```

```python
import functools

import jax
import jax.numpy as jnp
from jax import lax
from jax.experimental import pallas as pl
from jax.experimental.pallas import tpu as pltpu
from jax.sharding import PartitionSpec as P

ITERS = 3
NA, NB = 4, 4
NK = NA * NB
NS = 32
MODES = 128
M = NK * MODES
MESH = pl.DeviceIdType.MESH

def kernel(
    occ_hbm, t0_hbm, warm_hbm, cour_hbm, sign_hbm, s_hbm,
    q_landed, tails,
    occ_ref, t0_ref, warm_ref, cour_ref, sign_ref,
    full, sent, state, q_sent, q_state, coef_sent, coefs, q_final, tail, lhs, wlhs, relax, xs, xr, zs, zr, moved, half,
    fetch_sem, kept_sem, own_sem, gz_send, gz_recv, gx_send, gx_recv, gf_send, gf_recv, gy_send, gy_recv, gp_send, gp_recv, c_send, c_recv, in_send, in_recv, x_send, x_recv, z_send, z_recv, o_send, o_recv,
):
    s = lax.axis_index("space")
    k = lax.axis_index("mode")
    a, b = k // NB, k % NB
    lo = s // 16
    core = s % 2

    def dev(space, mode):
        return {"space": space, "mode": mode}

    def wrap(v, n):
        return lax.rem(v + 4 * n, n)

    y = (s // 2) % 8
    toward = 2 * lo - 1
    z_near = dev(lax.rem(s + 16, NS), wrap(a + toward, NA) * NB + b)
    z_over = dev(s, wrap(a + toward, NA) * NB + b)
    z_back = dev(s, wrap(a - toward, NA) * NB + b)
    x_up, x_down = dev(s, a * NB + wrap(b + 1, NB)), dev(s, a * NB + wrap(b - 1, NB))
    z_pair = dev(lax.rem(s + 16, NS), k)
    y_up = dev(lo * 16 + wrap(y + 1, 8) * 2 + core, k)
    y_down = dev(lo * 16 + wrap(y - 1, 8) * 2 + core, k)
    partner = dev(s + 1 - 2 * core, k)
    right, left = dev(wrap(s + 1, NS), k), dev(wrap(s - 1, NS), k)

    def block_of(mode):
        aa, bb = mode // NB, mode % NB
        return aa * NB + bb + (aa % 2) * (NB - 1 - 2 * bb)

    zb = block_of(k)
    z_next, z_prev = dev(s, block_of(wrap(zb + 1, NK))), dev(s, block_of(wrap(zb - 1, NK)))

    def mode_peer(d):
        return wrap(k + d, NK)

    fetches = [
        pltpu.make_async_copy(src, dst, fetch_sem.at[i])
        for i, (src, dst) in enumerate((
            (occ_hbm, occ_ref), (t0_hbm, t0_ref), (warm_hbm, warm_ref), (cour_hbm, cour_ref), (sign_hbm, sign_ref),
        ))
    ]
    for fetch in fetches:
        fetch.start()
    own = pltpu.make_async_copy(s_hbm, full.at[a, b], own_sem)
    own.start()
    barrier = pltpu.get_barrier_semaphore()

    for peer in (right, left, z_near, z_pair, y_up, y_down):
        pl.semaphore_signal(barrier, inc=1, device_id=peer, device_id_type=MESH)

    @pl.loop(1, NK, unroll=3)
    def _(d):
        pl.semaphore_signal(barrier, inc=1, device_id=dev(s, mode_peer(d)), device_id_type=MESH)

    pl.semaphore_wait(barrier, NK - 1 + 6)

    own.wait()
    rows = [a, wrap(a + toward, NA), wrap(a - toward, NA), wrap(a + 2, NA)]
    cols = [b, wrap(b - 1, NB), wrap(b + 1, NB), wrap(b + 2, NB)]
    parity = lax.rem(y + lo, 2)
    mine_u = parity * 4 + core * 2
    other_u = (1 - parity) * 4 + core * 2
    started = []

    def remote(block, send, recv, peer):
        return pltpu.make_async_remote_copy(
            src_ref=block, dst_ref=block, send_sem=send, recv_sem=recv, device_id=peer, device_id_type=MESH
        )

    def z_copy(n):
        block = full.at[rows[1] if n == 3 else a, b, pl.ds(other_u if n == 1 else mine_u, 2)]
        return remote(block, gz_send.at[n], gz_recv.at[n], (z_near, z_over, z_back)[n - 1])

    def x_copy(n, way):
        block = full.at[rows[n], b, pl.ds(mine_u, 2)]
        return remote(block, gx_send.at[n, way], gx_recv.at[n, way], x_down if way else x_up)

    def far_copy(n, way):
        block = full.at[rows[n], cols[1 + way], mine_u + way]
        return remote(block, gf_send.at[n, way], gf_recv.at[n, way], x_down if way else x_up)

    def y_copy(n, m, way):
        block = full.at[rows[n], cols[m], mine_u + way]
        return remote(block, gy_send.at[n, m, way], gy_recv.at[n, m, way], y_down if way else y_up)

    def pair_copy(n, m):
        there = (0, 2, 1, 3)[n]
        return remote(full.at[rows[n], cols[m], pl.ds(mine_u, 2)], gp_send.at[n, m], gp_recv.at[there, m], z_pair)

    def core_copy(n, m, kind):
        block = full.at[rows[n], cols[m], pl.ds(other_u if kind else mine_u, 2)]
        return remote(block, c_send.at[n, m, kind], c_recv.at[n, m, kind], partner)

    def start(copy):
        copy.start()
        started.append(copy)

    def share(n, m):
        if m == 1:
            start(pair_copy(n, m))
        else:
            start(y_copy(n, m, 0))
            start(y_copy(n, m, 1))
        start(core_copy(n, m, 0))

    start(z_copy(1))
    start(x_copy(0, 0))
    start(x_copy(0, 1))
    start(z_copy(2))


    def a2a(pairs, send, recv, d):
        return [
            pltpu.make_async_remote_copy(
                src_ref=src, dst_ref=dst, send_sem=send.at[d, i], recv_sem=recv.at[d, i],
                device_id=dev(s, mode_peer(d)), device_id_type=MESH,
            )
            for i, (src, dst) in enumerate(pairs)
        ]

    def a2a_in(d):
        block = block_of(mode_peer(d))
        pairs = (q_sent.at[block], q_state.at[k]), (coef_sent.at[block], coefs.at[k])
        return a2a(pairs, in_send, in_recv, d)

    def a2a_out(d):
        there = mode_peer(d)
        pairs = (q_final.at[there], q_landed.at[zb]), (tail.at[there], tails.at[zb])
        return a2a(pairs, o_send, o_recv, d)

    def quantized(values):
        most = jnp.max(jnp.abs(values), axis=0, keepdims=True)
        steps = jnp.where(most > 0.0, 32767.0 / most, 0.0)
        return jnp.round(values * steps).astype(jnp.int32).astype(jnp.int16), most * (1.0 / 32767.0)

    for fetch in fetches:
        fetch.wait()

    warm_col = jnp.transpose(jnp.broadcast_to(warm_ref[pl.ds(k, 1), :], (MODES, MODES)))
    for xy in range(8):
        cells = occ_ref[pl.ds(xy, MODES, stride=8), :] + warm_col * t0_ref[xy:xy + 1, :]
        sent[:, pl.ds(xy * 8, 8), :] = jnp.transpose(cells).reshape(NK, 8, MODES)
    sign = sign_ref[...]
    row = lax.broadcasted_iota(jnp.int32, (8, MODES), 0)
    coef = jnp.zeros((8, MODES), jnp.float32)
    for d in range(3):
        bit = jnp.broadcast_to((sign >> d) & 1, (8, MODES))
        c = jnp.broadcast_to(cour_ref[d:d + 1, :], (8, MODES))
        coef = jnp.where(row == 2 * d, jnp.where(bit == 0, c, 0.0), coef)
        coef = jnp.where(row == 2 * d + 1, jnp.where(bit == 1, c, 0.0), coef)

    @pl.loop(0, NK, unroll=4)
    def _(j):
        q, step = quantized(sent[j])
        q_sent[j] = q
        coef_sent[j] = jnp.where(row == 6, jnp.broadcast_to(step, (8, MODES)), coef)

    q_state[k] = q_sent[zb]
    coefs[k] = coef_sent[zb]

    def from_z(n):
        z_copy(n).wait_recv()
        if n == 1:
            start(z_copy(3))
        start(x_copy(n, 0))
        start(x_copy(n, 1))
        share(n, 0)

    def from_x(n):
        for way in range(2):
            x_copy(n, way).wait_recv()
            start(far_copy(n, way))
        share(n, 1)
        share(n, 2)

    def from_far_x(n):
        far_copy(n, 0).wait_recv()
        far_copy(n, 1).wait_recv()
        share(n, 3)

    def from_others(n):
        for m in range(4):
            if n or m:
                if m == 1:
                    pair_copy((0, 2, 1, 3)[n], m).wait_recv()
                else:
                    y_copy(n, m, 0).wait_recv()
                    y_copy(n, m, 1).wait_recv()
                start(core_copy(n, m, 1))

    from_z(1)
    from_x(0)

    @pl.loop(1, NK, unroll=3)
    def _(d):
        for copy in a2a_in(lax.rem(d + 6, NK - 1) + 1):
            copy.start()

    from_z(2)
    from_far_x(0)
    from_x(1)
    from_z(3)
    from_x(2)
    from_far_x(1)
    from_others(0)

    total = jnp.sum(warm_ref[...])
    zi = lax.broadcasted_iota(jnp.int32, (8, 8, MODES), 1)
    nt = (((1,), (1,)), ((), ()))

    def halo_copies(t, h):
        part = pl.ds(h * NB, NB)
        return [
            pltpu.make_async_remote_copy(
                src_ref=src.at[t, way, part], dst_ref=dst.at[t, way, part],
                send_sem=send.at[t, way, h], recv_sem=recv.at[t, way, h], device_id=peer, device_id_type=MESH,
            )
            for src, dst, send, recv, peers in (
                (xs, xr, x_send, x_recv, (right, left)), (zs, zr, z_send, z_recv, (z_next, z_prev)),
            )
            for way, peer in enumerate(peers)
        ]

    def stage_halo(t, j):
        xs[t, 0, j] = state[j, 32:64, :].astype(jnp.bfloat16)
        xs[t, 1, j] = state[j, 0:32, :].astype(jnp.bfloat16)
        zs[t, 0, j] = state[j, pl.ds(7, 8, stride=8), :]
        zs[t, 1, j] = state[j, pl.ds(0, 8, stride=8), :]

    def send_halo(t, h):
        for copy in halo_copies(t, h):
            copy.start()

    def advect_block(t, j, energy):
        st = state[j].reshape(8, 8, MODES)
        cf = [coefs[j, pl.ds(r, 1), :].reshape(1, 1, MODES) for r in range(6)]
        below = xr[t, 0, j].astype(jnp.float32).reshape(4, 8, MODES)
        above = xr[t, 1, j].astype(jnp.float32).reshape(4, 8, MODES)
        x_below = jnp.concatenate([below, st[0:4]], axis=0)
        x_above = jnp.concatenate([st[4:8], above], axis=0)
        y_below = jnp.concatenate([st[3:4], st[0:3], st[7:8], st[4:7]], axis=0)
        y_above = jnp.concatenate([st[1:4], st[0:1], st[5:8], st[4:5]], axis=0)
        z_lower = zr[t, 0, j].reshape(8, 1, MODES)
        z_upper = zr[t, 1, j].reshape(8, 1, MODES)
        z_below = jnp.where(zi == 0, z_lower, jnp.roll(st, 1, 1))
        z_above = jnp.where(zi == 7, z_upper, jnp.roll(st, -1, 1))
        mv = st
        for d, (lower, upper) in enumerate(((x_below, x_above), (y_below, y_above), (z_below, z_above))):
            mv = mv - (cf[2 * d] * (st - lower) + cf[2 * d + 1] * (st - upper))
        mv = mv.reshape(64, MODES)
        mv_bf = mv.astype(jnp.bfloat16)
        moved[j] = mv
        lhs[:, pl.ds(pl.multiple_of(j * MODES, MODES), MODES)] = mv_bf
        return energy + mv_bf.astype(jnp.float32) * warm_ref[pl.ds(j, 1), :]

    def advect(t, h, energy):
        for q in range(2 * h, 2 * h + 2):
            for copy in halo_copies(t, q):
                copy.wait_recv()
            energy = lax.fori_loop(q * NB, q * NB + NB, functools.partial(advect_block, t), energy, unroll=4)
        return energy

    def offset(energy):
        thermal = jnp.sum(energy, axis=1, keepdims=True) / total
        return jnp.broadcast_to(thermal, (64, MODES))

    nothing = jnp.zeros((64, MODES), jnp.float32)

    row16 = lax.broadcasted_iota(jnp.int32, (16, MODES), 0)
    for j in range(NK):
        w = jnp.broadcast_to(warm_ref[j:j + 1, :], (16, MODES))
        hi = w.astype(jnp.bfloat16).astype(jnp.float32)
        mid = (w - hi).astype(jnp.bfloat16).astype(jnp.float32)
        low = w - hi - mid
        parts = jnp.where(row16 == 0, hi, jnp.where(row16 == 1, mid, jnp.where(row16 == 2, low, 0.0)))
        wlhs[:, j * MODES:(j + 1) * MODES] = parts.astype(jnp.bfloat16)

    @pl.loop(1, NK, unroll=3)
    def _(d):
        for copy in a2a_in(d):
            copy.wait_recv()

    @pl.loop(0, NA)
    def _(q):
        @pl.loop(0, NB, unroll=4)
        def _(e):
            j = q * NB + e
            state[j] = restored(q_state[j], coefs[j, 6:7])
            stage_halo(0, j)

        send_halo(0, q)

    from_x(3)
    from_far_x(2)
    from_others(1)
    from_far_x(3)
    thermal = offset(advect(0, 1, advect(0, 0, nothing)))

    def first_product(n):
        for m in range(4):
            if n or m:
                core_copy(n, m, 0).wait_recv()
                core_copy(n, m, 1).wait_recv()
        r = rows[n]
        w = full[r].reshape(4 * MODES, M)
        product = lax.dot_general(lhs[...], w, nt, preferred_element_type=jnp.float32)
        parts = lax.dot_general(wlhs[...], w, nt, preferred_element_type=jnp.float32)
        both = parts[0:1] + parts[1:2] + parts[2:3]
        for e in range(NB):
            j = r * NB + e
            rx = jnp.broadcast_to(both[:, e * MODES:(e + 1) * MODES], (8, MODES))
            relax[j] = rx
            state[j] = moved[j] - product[:, e * MODES:(e + 1) * MODES] + rx[0:1] * thermal
            stage_halo(1, j)
        send_halo(1, r)

    first_product(0)
    from_others(2)
    first_product(1)
    first_product(2)
    from_others(3)
    first_product(3)


    def halos_left(t):
        for q in range(NA):
            for copy in halo_copies(t, q):
                copy.wait_send()

    for copy in started:
        copy.wait_send()

    @pl.loop(1, NK, unroll=3)
    def _(d):
        for copy in a2a_in(d):
            copy.wait_send()

    halos_left(0)

    for t in range(1, ITERS):
        last = t == ITERS - 1
        if t > 1:
            halos_left(t - 1)
        energy = advect(t, 0, nothing)
        order = [cols[3], cols[2], cols[1], b] if last else list(range(NB))

        def weights(n, h):
            part = slice(h * (M // 2), (h + 1) * (M // 2))
            return jnp.concatenate([full[n, c, :, :, part].reshape(MODES, M // 2) for c in order], axis=0)

        @pl.loop(0, NA, unroll=2)
        def _(n):
            w = weights(n, 0)
            half[n] = lax.dot_general(lhs[:, 0:M // 2], w, nt, preferred_element_type=jnp.float32)

        thermal = offset(advect(t, 1, energy))
        if last:
            lane = lax.broadcasted_iota(jnp.int32, (64, MODES), 1)
            cell = lax.broadcasted_iota(jnp.int32, (64, MODES), 0)
            offsets = jnp.sum(jnp.where(lane == cell, thermal, 0.0), axis=0, keepdims=True)

        def finish(n, own_row=False):
            w = weights(n, 1)
            product = half[n] + lax.dot_general(lhs[:, M // 2:M], w, nt, preferred_element_type=jnp.float32)
            for e in range(NB):
                j = NB * n + order[e]
                new = moved[j] - product[:, e * MODES:(e + 1) * MODES] + relax[j, 0:1] * thermal
                if last:
                    q, step = quantized(new)
                    q_final[j] = q
                    tail[j] = jnp.concatenate([offsets, step], axis=0)
                    if not (own_row and e == NB - 1):
                        for copy in a2a_out(lax.rem(j - k + NK, NK)):
                            copy.start()
                else:
                    state[j] = new
                    stage_halo(t + 1, j)

        if last:
            for step in (2, 1, 3, 0):
                finish(wrap(a + step, NA), step == 0)
        else:
            @pl.loop(0, NA, unroll=2)
            def _(n):
                finish(n)
                send_halo(t + 1, n)

    kept = [
        pltpu.make_async_copy(q_final.at[k], q_landed.at[zb], kept_sem.at[0]),
        pltpu.make_async_copy(tail.at[k], tails.at[zb], kept_sem.at[1]),
    ]
    for copy in kept:
        copy.start()
    halos_left(ITERS - 1)
    for copy in kept:
        copy.wait()

    @pl.loop(1, NK, unroll=3)
    def _(d):
        for copy in a2a_out(d):
            copy.wait_recv()

    @pl.loop(1, NK, unroll=3)
    def _(d):
        for copy in a2a_out(d):
            copy.wait_send()


def restored(q, step):
    return q.astype(jnp.int32).astype(jnp.float32) * step


def unpack(q_ref, tail_ref, out_ref, therm_ref, back):
    @pl.loop(0, NK, unroll=8)
    def _(j):
        back[j] = restored(q_ref[j], tail_ref[j, 1:2]).reshape(8, 8, MODES)

    for xy in range(8):
        cells = back[:, xy].reshape(MODES, MODES)
        out_ref[pl.ds(xy, MODES, stride=8), :] = jnp.transpose(cells)
    lane = lax.broadcasted_iota(jnp.int32, (8, MODES), 1)
    offsets = jnp.zeros((8, MODES), jnp.float32)
    for j in range(NK):
        cells = jnp.broadcast_to(tail_ref[j, 0:1], (8, MODES))
        moved = pltpu.roll(cells, (8 * j - 56) % MODES, 1)
        moved = pltpu.roll(moved, 0, 1, stride=8, stride_axis=0)
        offsets = jnp.where(lane // 8 == j, moved, offsets)
    for xy in range(8):
        therm_ref[xy:xy + 1, :] = offsets[7 - xy:8 - xy]


def shards(occupation, offset, warmth, courant, sign, matrix):
    f32, bf16 = jnp.float32, jnp.bfloat16
    dma = pltpu.SemaphoreType.DMA
    vmem = pl.BlockSpec(memory_space=pltpu.VMEM)
    hbm = pl.BlockSpec(memory_space=pltpu.HBM)
    landed, tails = pl.pallas_call(
        kernel,
        out_shape=(
            jax.ShapeDtypeStruct((NK, 64, MODES), jnp.int16),
            jax.ShapeDtypeStruct((NK, 2, MODES), f32),
        ),
        in_specs=[hbm] * 6,
        out_specs=(hbm, hbm),
        scratch_shapes=[
            pltpu.VMEM((8 * MODES, 128), f32),
            pltpu.VMEM((8, 128), f32),
            pltpu.VMEM((NK, MODES), f32),
            pltpu.VMEM((3, MODES), f32),
            pltpu.VMEM((1, MODES), jnp.int32),
            pltpu.VMEM((NA, NB, 8, 16, M), bf16),
            pltpu.VMEM((NK, 64, MODES), f32),
            pltpu.VMEM((NK, 64, MODES), f32),
            pltpu.VMEM((NK, 64, MODES), jnp.int16),
            pltpu.VMEM((NK, 64, MODES), jnp.int16),
            pltpu.VMEM((NK, 8, MODES), f32),
            pltpu.VMEM((NK, 8, MODES), f32),
            pltpu.VMEM((NK, 64, MODES), jnp.int16),
            pltpu.VMEM((NK, 2, MODES), f32),
            pltpu.VMEM((64, M), bf16),
            pltpu.VMEM((16, M), bf16),
            pltpu.VMEM((NK, 8, MODES), f32),
            pltpu.VMEM((ITERS, 2, NK, 32, MODES), bf16),
            pltpu.VMEM((ITERS, 2, NK, 32, MODES), bf16),
            pltpu.VMEM((ITERS, 2, NK, 8, MODES), f32),
            pltpu.VMEM((ITERS, 2, NK, 8, MODES), f32),
            pltpu.VMEM((NK, 64, MODES), f32),
            pltpu.VMEM((NA, 64, NB * MODES), f32),
            dma((5,)),
            dma((2,)),
            dma,
            dma((4,)), dma((4,)),
            dma((4, 2)), dma((4, 2)),
            dma((4, 2)), dma((4, 2)),
            dma((4, 4, 2)), dma((4, 4, 2)),
            dma((4, 4)), dma((4, 4)),
            dma((4, 4, 2)), dma((4, 4, 2)),
            dma((NK, 2)), dma((NK, 2)),
            dma((ITERS, 2, NA)), dma((ITERS, 2, NA)),
            dma((ITERS, 2, NA)), dma((ITERS, 2, NA)),
            dma((NK, 2)), dma((NK, 2)),
        ],
        compiler_params=pltpu.CompilerParams(
            collective_id=0, has_side_effects=True, vmem_limit_bytes=62 * 1024 * 1024
        ),
        cost_estimate=pl.CostEstimate(flops=1_700_000_000, bytes_accessed=2_000_000, transcendentals=0),
    )(
        occupation.reshape(8 * MODES, 128),
        offset.reshape(8, 128),
        warmth.reshape(NK, MODES),
        courant,
        sign.reshape(1, MODES),
        matrix.reshape(8, 16, M),
    )
    out, therm = pl.pallas_call(
        unpack,
        out_shape=(
            jax.ShapeDtypeStruct((8 * MODES, 128), f32),
            jax.ShapeDtypeStruct((8, 128), f32),
        ),
        in_specs=[vmem, vmem],
        out_specs=(vmem, vmem),
        scratch_shapes=[pltpu.VMEM((NK, 8, 8, MODES), f32)],
    )(landed, tails)
    return out.reshape(occupation.shape), therm.reshape(offset.shape)


def solution(mesh):
    placed = (
        P("mode", "space", None, None),
        P("space", None, None),
        P(),
        P(None, "mode"),
        P("mode"),
        P("mode", None),
    )
    return jax.shard_map(
        shards,
        mesh=mesh,
        in_specs=placed,
        out_specs=(P("mode", "space", None, None), P("space", None, None)),
        check_vma=False,
    )
```
